256 devices in a mesh: seq: 64 (over x, y, z_hi), head: 4 (over z_lo, core).
Axes of the slice: x: 4, y: 4, z: 8 (z_hi: 4, z_lo: 2; z = z_hi * 2 + z_lo), core: 2. Of those that a mesh axis runs over, the one named last changes fastest.
Arguments:
- query: bfloat16 [32768, 4096], P('seq', 'head'), may hold values from -6 to 6
- comp_key: bfloat16 [32768, 1024], P('seq', 'head'), may hold values from -6 to 6
- comp_value: bfloat16 [32768, 1024], P('seq', 'head'), may hold values from -6 to 6
- prompt_key: bfloat16 [2048, 1024], P(('seq', 'head')), may hold values from -6 to 6
- prompt_value: bfloat16 [2048, 1024], P(('seq', 'head')), may hold values from -6 to 6
- out_grad: bfloat16 [32768, 4096], P('seq', 'head'), may hold values from -16 to 16
- row_comp: int32 [32768], P('seq'), may hold values from 0 to 127, as said below
- prompt_owner: int32 [8], replicated, may hold values from 0 to 7, each once
Outputs:
- attn_out: bfloat16 [32768, 4096], P('seq', 'head')
- query_grad: bfloat16 [32768, 4096], P('seq', 'head')
- key_grad: bfloat16 [32768, 1024], P('seq', 'head')
- value_grad: bfloat16 [32768, 1024], P('seq', 'head')
- prompt_key_grad: bfloat16 [2048, 1024], P(('seq', 'head'))
- prompt_value_grad: bfloat16 [2048, 1024], P(('seq', 'head'))
The draws below stay inside these ranges and needn't reach their ends.
Inputs may be any that keep to these rules, and one draw needn't show every extreme that they name: `row_comp`: each aligned block of 512 rows holds exactly two different completions, each as one run of one or more rows; every completion lies in exactly one block. A permutation: prompt p sits in slot prompt_owner[p].
All inputs are finite; a program needn't handle non-finite values.
Results may differ from the reference program's by a relative error of at most 0.025.
Values may be sent and summed in bfloat16 or wider, within the bound.
A program may use at most 128 MiB of HBM per device.

```python
import math
import jax
import jax.numpy as jnp
from jax import lax

QH = 32
KVH = 8
HD = 128
NPROMPT = 8
PLEN = 256
ROWS_DEV = 512
TOKENS = 32768
NGEN = 16
PROWS = 2048


def draw_query(key, part):
    key = jax.random.fold_in(key, 11)
    drawn = jnp.clip(jax.random.normal(key, (TOKENS, QH * HD), jnp.float32), -6.0, 6.0)
    return drawn.astype(jnp.bfloat16)


def draw_comp_key(key, part):
    key = jax.random.fold_in(key, 12)
    drawn = jnp.clip(jax.random.normal(key, (TOKENS, KVH * HD), jnp.float32), -6.0, 6.0)
    return drawn.astype(jnp.bfloat16)


def draw_row_comp(key, part):
    key = jax.random.fold_in(key, 13)
    key_order, key_split = jax.random.split(key)
    blocks = TOKENS // ROWS_DEV
    comp_order = jax.random.permutation(key_order, 2 * blocks)
    split_at = jax.random.randint(key_split, (blocks,), 1, ROWS_DEV)
    row_number = jnp.arange(TOKENS)
    device = row_number // ROWS_DEV
    local_row = row_number % ROWS_DEV
    lead_comp = comp_order[2 * device]
    tail_comp = comp_order[2 * device + 1]
    return jnp.where(local_row < split_at[device], lead_comp, tail_comp).astype(jnp.int32)


def block_levels(stream_key, shape, shards, low, top_value):
    def one(position, parts):
        steps = jax.random.uniform(jax.random.fold_in(jax.random.fold_in(stream_key, 6), position), (parts,), jnp.float32, low / len(shards), top_value / len(shards))
        return jnp.repeat(jnp.exp(steps), shape[position] // parts).reshape((-1,) + (1,) * (len(shape) - position - 1))

    factor_of = one(*shards[0])
    for cut in shards[1:]:
        factor_of = factor_of * one(*cut)
    return factor_of


def noise(key, extent, width, bound, shards=(), held_as=jnp.bfloat16):
    result = jax.random.normal(key, extent, jnp.float32) * width
    if len(shards) > 0:
        result = block_levels(key, extent, shards, -0.22, 0.18) * result
    return jnp.clip(result, min=-bound, max=bound).astype(held_as)


def setup_inputs(seed: int = 0) -> dict:
    arg_keys = jax.random.split(jax.random.key(seed), 9)
    return {
        "query": draw_query(jax.random.fold_in(arg_keys[8], 71), 0),
        "comp_key": draw_comp_key(jax.random.fold_in(arg_keys[8], 71), 0),
        "comp_value": noise(arg_keys[2], (TOKENS, KVH * HD), 1.0, 6.0, ((0, 64), (1, 4))),
        "prompt_key": noise(arg_keys[3], (PROWS, KVH * HD), 1.0, 6.0, ((0, 256),)),
        "prompt_value": noise(arg_keys[4], (PROWS, KVH * HD), 1.0, 6.0, ((0, 256),)),
        "out_grad": noise(arg_keys[5], (TOKENS, QH * HD), 4.0, 16.0, ((0, 64), (1, 4))),
        "row_comp": draw_row_comp(jax.random.fold_in(arg_keys[8], 71), 0),
        "prompt_owner": jax.random.permutation(arg_keys[7], NPROMPT).astype(jnp.int32),
    }


NEG_FILL = -1e+30

def attend(query_part, key_part, value_part, grad_part, visible):
    inv_sqrt = 1.0 / math.sqrt(query_part.shape[-1])
    query_f = query_part.astype(jnp.float32)
    key_f = key_part.astype(jnp.float32)
    value_f = value_part.astype(jnp.float32)
    grad_f = grad_part.astype(jnp.float32)
    scores = jnp.einsum('rhgd,khd->hgrk', query_f, key_f) * inv_sqrt
    scores = jnp.where(visible[None, None], scores, NEG_FILL)
    row_max = lax.optimization_barrier(jnp.max(scores, axis=-1, keepdims=True))
    raw_weights = jnp.exp(scores - row_max)
    weights = raw_weights / lax.optimization_barrier(jnp.sum(raw_weights, axis=-1, keepdims=True))
    weights_half = lax.optimization_barrier(weights.astype(jnp.bfloat16))
    attended = jnp.einsum('hgrk,khd->rhgd', weights_half.astype(jnp.float32), value_f).astype(jnp.bfloat16)
    attended = lax.optimization_barrier(attended)
    row_delta = lax.optimization_barrier(jnp.sum(grad_f * attended.astype(jnp.float32), axis=-1))
    grad_weights = jnp.einsum('rhgd,khd->hgrk', grad_f, value_f)
    dscore = weights * (grad_weights - jnp.transpose(row_delta, (1, 2, 0))[..., None])
    dscore_half = lax.optimization_barrier(dscore.astype(jnp.bfloat16)).astype(jnp.float32)
    query_grads = (jnp.einsum('hgrk,khd->rhgd', dscore_half, key_f) * inv_sqrt).astype(jnp.bfloat16)
    key_grads = jnp.einsum('hgrk,rhgd->khd', dscore_half, query_f) * inv_sqrt
    value_grads = jnp.einsum('hgrk,rhgd->khd', weights_half.astype(jnp.float32), grad_f)
    return (attended, query_grads, key_grads, value_grads)

def add_at(running_sum, grad_piece, row_start):
    current = lax.dynamic_slice_in_dim(running_sum, row_start, grad_piece.shape[0], 0)
    return lax.dynamic_update_slice_in_dim(running_sum, current + grad_piece, row_start, 0)

def reference(query, comp_key, comp_value, prompt_key, prompt_value, out_grad, row_comp, prompt_owner):
    q_group = QH // KVH
    col_width = KVH * HD

    def one_block(running, block_index):
        key_total, value_total = running
        row_start = (block_index * ROWS_DEV).astype(jnp.int32)

        def rows_of(source):
            return lax.dynamic_slice_in_dim(source, row_start, ROWS_DEV, 0)
        block_query = rows_of(query).reshape(ROWS_DEV, KVH, q_group, HD)
        block_grad = rows_of(out_grad).reshape(ROWS_DEV, KVH, q_group, HD)
        block_comp = rows_of(row_comp)
        lead_comp = block_comp[0]
        tail_comp = block_comp[ROWS_DEV - 1]
        lead_row = (prompt_owner[lead_comp // NGEN] * PLEN).astype(jnp.int32)
        tail_row = (prompt_owner[tail_comp // NGEN] * PLEN).astype(jnp.int32)
        key_rows = jnp.concatenate([lax.dynamic_slice_in_dim(prompt_key, lead_row, PLEN, 0), lax.dynamic_slice_in_dim(prompt_key, tail_row, PLEN, 0), rows_of(comp_key)], 0).reshape(-1, KVH, HD)
        value_rows = jnp.concatenate([lax.dynamic_slice_in_dim(prompt_value, lead_row, PLEN, 0), lax.dynamic_slice_in_dim(prompt_value, tail_row, PLEN, 0), rows_of(comp_value)], 0).reshape(-1, KVH, HD)
        in_lead = block_comp == lead_comp
        positions = jnp.arange(ROWS_DEV)
        local_seen = (block_comp[:, None] == block_comp[None, :]) & (positions[:, None] >= positions[None, :])
        visible = jnp.concatenate([jnp.broadcast_to(in_lead[:, None], (ROWS_DEV, PLEN)), jnp.broadcast_to(jnp.logical_not(in_lead)[:, None], (ROWS_DEV, PLEN)), local_seen], 1)
        attended, query_grads, key_grads, value_grads = attend(block_query, key_rows, value_rows, block_grad, visible)
        key_grads = key_grads.reshape(-1, col_width)
        value_grads = value_grads.reshape(-1, col_width)
        key_total = add_at(key_total, key_grads[:PLEN], lead_row)
        key_total = add_at(key_total, key_grads[PLEN:2 * PLEN], tail_row)
        value_total = add_at(value_total, value_grads[:PLEN], lead_row)
        value_total = add_at(value_total, value_grads[PLEN:2 * PLEN], tail_row)
        outputs = (attended.reshape(ROWS_DEV, QH * HD), query_grads.reshape(ROWS_DEV, QH * HD), key_grads[2 * PLEN:].astype(jnp.bfloat16), value_grads[2 * PLEN:].astype(jnp.bfloat16))
        return ((key_total, value_total), outputs)
    zero_rows = jnp.zeros((PROWS, col_width), jnp.float32)
    totals, pieces = lax.scan(one_block, (zero_rows, zero_rows), jnp.arange(TOKENS // ROWS_DEV, dtype=jnp.int32))
    attn_out = pieces[0].reshape(TOKENS, QH * HD)
    query_grad = pieces[1].reshape(TOKENS, QH * HD)
    key_grad = pieces[2].reshape(TOKENS, col_width)
    value_grad = pieces[3].reshape(TOKENS, col_width)
    return (attn_out, query_grad, key_grad, value_grad, totals[0].astype(jnp.bfloat16), totals[1].astype(jnp.bfloat16))
```

```python
import functools
import math

import jax
import jax.numpy as jnp
from jax import lax
from jax.experimental import pallas as pl
from jax.experimental.pallas import tpu as pltpu
from jax.sharding import PartitionSpec as P

QH = 32
KVH = 8
HD = 128
NPROMPT = 8
PLEN = 256
NGEN = 16
ROWS = 512
GROUP = QH // KVH
HEADS = 4
PLANE = 16
DEPTH = 4
COLS = 256
CHUNK = 128
MESH = pl.DeviceIdType.MESH
INV_SQRT = 1.0 / math.sqrt(HD)
EXP2_SCALE = INV_SQRT * math.log2(math.e)
NEG_FILL = -1e30
F32 = jnp.float32
BF16 = jnp.bfloat16


def place():
    seq = lax.axis_index("seq")
    head = lax.axis_index("head")
    plane = seq // DEPTH
    z = lax.rem(seq, DEPTH)
    unit = 4 * lax.rem(seq, 8) + head
    return seq, head, plane, z, seq // 8, unit


def spread_target(unit, i):
    return (unit // 2) * DEPTH + lax.rem(i, DEPTH), i // DEPTH


def holder_of(plane, i):
    unit = 2 * plane + lax.rem(i, 2)
    return 8 * (i // 2) + unit // 4, lax.rem(unit, 4)


def entry_barrier(peers, spreads):
    seq, head, plane, z, slot, unit = place()
    barrier = pltpu.get_barrier_semaphore()

    def greet_peer(i, carry):
        other = lax.rem(plane + i, PLANE) * DEPTH + z
        pl.semaphore_signal(barrier, inc=1, device_id=(other, head), device_id_type=MESH)
        return carry

    def greet(i, carry):
        for other, other_head in (spread_target(unit, i), holder_of(plane, i)):
            @pl.when(jnp.logical_or(other != seq, other_head != head))
            def _():
                pl.semaphore_signal(barrier, inc=1, device_id=(other, other_head), device_id_type=MESH)
        return carry

    lax.fori_loop(1, PLANE, greet_peer, 0)
    lax.fori_loop(0, 16, greet, 0)
    own = unit // 2 == plane

    @pl.when(own)
    def _():
        pl.semaphore_wait(barrier, 15 + 30)

    @pl.when(jnp.logical_not(own))
    def _():
        pl.semaphore_wait(barrier, 15 + 32)


def wait_bytes(ref, sem):
    pltpu.make_async_copy(ref, ref, sem).wait()


def gather_kernel(
    owner_ref, comp_ref, key_ref, value_ref, out_ref, slots_ref,
    own_rows, dense, packed, picked, info, infos, infos_smem,
    send_a, recv_a, send_i, recv_i, send_b, recv_b, local_sem,
):
    seq, head, plane, z, slot, unit = place()
    entry_barrier(True, True)

    lead = owner_ref[comp_ref[0] // NGEN]
    tail = owner_ref[comp_ref[ROWS - 1] // NGEN]
    row = lax.broadcasted_iota(jnp.int32, (8, 128), 0)
    info[...] = jnp.where(row < 4, lead, tail)
    infos[plane] = info[...]

    both = jnp.concatenate([key_ref[...].astype(F32), value_ref[...].astype(F32)], 0).astype(BF16)
    for part in range(HEADS):
        own_rows[part] = both[:, part * COLS : (part + 1) * COLS]

    def copy_a(i):
        other, other_head = spread_target(unit, i)
        is_self = jnp.logical_and(other == seq, other_head == head)
        copy = pltpu.make_async_remote_copy(
            src_ref=own_rows.at[i // DEPTH], dst_ref=dense.at[2 * slot + lax.rem(unit, 2)],
            send_sem=send_a.at[i], recv_sem=recv_a.at[2 * slot + lax.rem(unit, 2)],
            device_id=(other, other_head), device_id_type=MESH,
        )
        return is_self, copy

    def start_a(i, carry):
        is_self, copy = copy_a(i)

        @pl.when(is_self)
        def _():
            pltpu.make_async_copy(
                own_rows.at[i // DEPTH], dense.at[2 * slot + lax.rem(unit, 2)],
                recv_a.at[2 * slot + lax.rem(unit, 2)],
            ).start()

        @pl.when(jnp.logical_not(is_self))
        def _():
            copy.start()

        return carry

    def copy_info(i):
        other = lax.rem(plane + i, PLANE)
        return pltpu.make_async_remote_copy(
            src_ref=info, dst_ref=infos.at[plane],
            send_sem=send_i.at[i], recv_sem=recv_i.at[plane],
            device_id=(other * DEPTH + z, head), device_id_type=MESH,
        )

    def start_info(i, carry):
        copy_info(i).start()
        return carry

    lax.fori_loop(1, PLANE, start_info, 0)
    lax.fori_loop(0, 16, start_a, 0)

    def wait_info(i, carry):
        other = lax.rem(plane + i, PLANE)
        wait_bytes(infos.at[other], recv_i.at[other])
        return carry

    lax.fori_loop(1, PLANE, wait_info, 0)
    to_smem = pltpu.make_async_copy(infos, infos_smem, local_sem)
    to_smem.start()

    def wait_a(i, carry):
        wait_bytes(dense.at[i], recv_a.at[i])
        return carry

    lax.fori_loop(0, 16, wait_a, 0)
    to_smem.wait()
    for p in range(NPROMPT):
        first = dense[2 * p].astype(F32)
        second = dense[2 * p + 1].astype(F32)
        packed[p, 0] = jnp.concatenate([first[:8], second[:8]], 0).astype(BF16)
        packed[p, 1] = jnp.concatenate([first[8:], second[8:]], 0).astype(BF16)

    def copy_b(i):
        other = lax.rem(plane + i, PLANE)
        return pltpu.make_async_remote_copy(
            src_ref=picked.at[i], dst_ref=out_ref.at[plane],
            send_sem=send_b.at[i], recv_sem=recv_b.at[plane],
            device_id=(other * DEPTH + z, head), device_id_type=MESH,
        )

    def start_b(i, carry):
        other = lax.rem(plane + i, PLANE)
        picked[i, 0] = packed[infos_smem[other, 0, 0]]
        picked[i, 1] = packed[infos_smem[other, 4, 0]]
        copy_b(i).start()
        return carry

    lax.fori_loop(1, PLANE, start_b, 0)
    out_ref[plane, 0] = packed[lead]
    out_ref[plane, 1] = packed[tail]

    def note_slot(i, carry):
        slots_ref[2 * i] = infos_smem[i, 0, 0]
        slots_ref[2 * i + 1] = infos_smem[i, 4, 0]
        return carry

    lax.fori_loop(0, PLANE, note_slot, 0)

    def wait_b(i, carry):
        other = lax.rem(plane + i, PLANE)
        wait_bytes(out_ref.at[other], recv_b.at[other])
        return carry

    lax.fori_loop(1, PLANE, wait_b, 0)

    def wait_sends(i, carry):
        copy_info(i).wait_send()
        copy_b(i).wait_send()
        return carry

    lax.fori_loop(1, PLANE, wait_sends, 0)

    def wait_send_a(i, carry):
        is_self, copy = copy_a(i)

        @pl.when(jnp.logical_not(is_self))
        def _():
            copy.wait_send()

        return carry

    lax.fori_loop(0, 16, wait_send_a, 0)


def reduce_kernel(
    slots_ref, part_ref, key_out, value_out,
    parts, pieces, finals, send_b, recv_b, send_a, recv_a,
):
    seq, head, plane, z, slot, unit = place()
    entry_barrier(True, True)

    def copy_b(i):
        other = lax.rem(plane + i, PLANE)
        return pltpu.make_async_remote_copy(
            src_ref=part_ref.at[other], dst_ref=parts.at[plane],
            send_sem=send_b.at[i], recv_sem=recv_b.at[plane],
            device_id=(other * DEPTH + z, head), device_id_type=MESH,
        )

    def start_b(i, carry):
        copy_b(i).start()
        return carry

    lax.fori_loop(1, PLANE, start_b, 0)
    parts[plane] = part_ref[plane]

    lane = lax.broadcasted_iota(jnp.int32, (1, 2 * PLANE * 16), 1)
    lane_slot = jnp.zeros((1, 2 * PLANE * 16), jnp.int32)
    for i in range(2 * PLANE):
        lane_slot = jnp.where(lane // 16 == i, slots_ref[i], lane_slot)
    row = lax.broadcasted_iota(jnp.int32, (NPROMPT * 16, 2 * PLANE * 16), 0)
    lanes = lax.broadcasted_iota(jnp.int32, (NPROMPT * 16, 2 * PLANE * 16), 1)
    chosen = jnp.logical_and(row // 16 == lane_slot, lax.rem(row, 16) == lax.rem(lanes, 16))
    chosen = jnp.where(chosen, 1.0, 0.0).astype(BF16)

    def wait_b(i, carry):
        other = lax.rem(plane + i, PLANE)
        wait_bytes(parts.at[other], recv_b.at[other])
        return carry

    lax.fori_loop(1, PLANE, wait_b, 0)
    sums = [
        jnp.dot(chosen, parts[:, :, kv].reshape(2 * PLANE * 16, COLS), preferred_element_type=F32)
        for kv in range(2)
    ]
    for p in range(NPROMPT):
        for k in range(2):
            lo = 16 * p + 8 * k
            pieces[2 * p + k] = jnp.concatenate([sums[0][lo : lo + 8], sums[1][lo : lo + 8]], 0).astype(BF16)

    def copy_a(i):
        other, other_head = holder_of(plane, i)
        is_self = jnp.logical_and(other == seq, other_head == head)
        copy = pltpu.make_async_remote_copy(
            src_ref=pieces.at[i], dst_ref=finals.at[DEPTH * head + z],
            send_sem=send_a.at[i], recv_sem=recv_a.at[DEPTH * head + z],
            device_id=(other, other_head), device_id_type=MESH,
        )
        return is_self, copy

    def start_a(i, carry):
        is_self, copy = copy_a(i)

        @pl.when(is_self)
        def _():
            pltpu.make_async_copy(
                pieces.at[i], finals.at[DEPTH * head + z], recv_a.at[DEPTH * head + z]
            ).start()

        @pl.when(jnp.logical_not(is_self))
        def _():
            copy.start()

        return carry

    lax.fori_loop(0, 16, start_a, 0)

    def wait_a(i, carry):
        wait_bytes(finals.at[i], recv_a.at[i])
        return carry

    lax.fori_loop(0, 16, wait_a, 0)
    for part in range(HEADS):
        total = finals[DEPTH * part].astype(F32)
        for other_z in range(1, DEPTH):
            total = total + finals[DEPTH * part + other_z].astype(F32)
        key_out[:, part * COLS : (part + 1) * COLS] = total[:8].astype(BF16)
        value_out[:, part * COLS : (part + 1) * COLS] = total[8:].astype(BF16)

    def wait_sends(i, carry):
        copy_b(i).wait_send()
        return carry

    lax.fori_loop(1, PLANE, wait_sends, 0)

    def wait_send_a(i, carry):
        is_self, copy = copy_a(i)

        @pl.when(jnp.logical_not(is_self))
        def _():
            copy.wait_send()

        return carry

    lax.fori_loop(0, 16, wait_send_a, 0)


def dot(a, b):
    return jnp.dot(a, b, preferred_element_type=F32)


def attend_kernel(
    comp_ref, q_ref, k_ref, v_ref, kv_ref, g_ref,
    out_ref, qg_ref, kg_ref, vg_ref, part_ref,
    w_prompt, d_prompt, w_local, d_local,
):
    lead_rows = comp_ref[...] == comp_ref[0, 0]
    split = jnp.sum(jnp.where(lead_rows, 1.0, 0.0)).astype(jnp.int32)
    key_pair = jnp.concatenate([kv_ref[:, t, 0].reshape(PLEN, HD) for t in range(2)], 1)
    value_pair = jnp.concatenate([kv_ref[:, t, 1].reshape(PLEN, HD) for t in range(2)], 1)
    key_pair_t = key_pair.T
    value_pair_t = value_pair.T
    keys_t = k_ref[...].T
    values_t = v_ref[...].T
    for chunk in range(ROWS // CHUNK):
        lo, hi = chunk * CHUNK, (chunk + 1) * CHUNK
        span = slice(chunk * GROUP * CHUNK, (chunk + 1) * GROUP * CHUNK)
        q_t = jnp.concatenate([q_ref[lo:hi, j * HD : (j + 1) * HD].T for j in range(GROUP)], 1)
        g_t = jnp.concatenate([g_ref[lo:hi, j * HD : (j + 1) * HD].T for j in range(GROUP)], 1)
        row = lo + lax.broadcasted_iota(jnp.int32, (1, GROUP * CHUNK), 1) % CHUNK
        is_lead = row < split
        zero = jnp.zeros_like(q_t)
        q_pair_t = jnp.concatenate([jnp.where(is_lead, q_t, zero), jnp.where(is_lead, zero, q_t)], 0)
        g_pair_t = jnp.concatenate([jnp.where(is_lead, g_t, zero), jnp.where(is_lead, zero, g_t)], 0)
        key_at = lax.broadcasted_iota(jnp.int32, (hi, CHUNK), 0)
        row_at = lo + lax.broadcasted_iota(jnp.int32, (hi, CHUNK), 1)
        seen = jnp.logical_and(key_at <= row_at, jnp.logical_or(key_at >= split, row_at < split))
        bias = jnp.where(seen, 0.0, NEG_FILL)
        bias = jnp.concatenate([bias] * GROUP, 1)
        s_prompt = dot(key_pair, q_pair_t)
        s_local = dot(k_ref[:hi], q_t) + bias
        top = jnp.maximum(
            jnp.max(s_prompt, axis=0, keepdims=True), jnp.max(s_local, axis=0, keepdims=True)
        )
        e_prompt = jnp.exp2((s_prompt - top) * EXP2_SCALE)
        e_local = jnp.exp2((s_local - top) * EXP2_SCALE)
        total = jnp.sum(e_prompt, axis=0, keepdims=True) + jnp.sum(e_local, axis=0, keepdims=True)
        inv = 1.0 / total
        e_prompt = e_prompt * inv
        e_local = e_local * inv
        wh_prompt = e_prompt.astype(BF16)
        wh_local = e_local.astype(BF16)
        w_prompt[:, span] = wh_prompt
        w_local[:hi, span] = wh_local
        o_pair = dot(value_pair_t, wh_prompt)
        o_t = jnp.where(is_lead, o_pair[:HD], o_pair[HD:]) + dot(values_t[:, :hi], wh_local)
        o_t = o_t.astype(BF16).astype(F32)
        delta = jnp.sum(o_t * g_t.astype(F32), axis=0, keepdims=True)
        ds_prompt = (e_prompt * (dot(value_pair, g_pair_t) - delta)).astype(BF16)
        ds_local = (e_local * (dot(v_ref[:hi], g_t) - delta)).astype(BF16)
        d_prompt[:, span] = ds_prompt
        d_local[:hi, span] = ds_local
        dq_pair = dot(key_pair_t, ds_prompt)
        dq_t = jnp.where(is_lead, dq_pair[:HD], dq_pair[HD:]) + dot(keys_t[:, :hi], ds_local)
        dq_t = dq_t * INV_SQRT
        for j in range(GROUP):
            out_ref[lo:hi, j * HD : (j + 1) * HD] = o_t[:, j * CHUNK : (j + 1) * CHUNK].T.astype(BF16)
            qg_ref[lo:hi, j * HD : (j + 1) * HD] = dq_t[:, j * CHUNK : (j + 1) * CHUNK].T.astype(BF16)

    def stacked(ref):
        return jnp.concatenate(
            [
                ref[c * CHUNK : (c + 1) * CHUNK, j * HD : (j + 1) * HD]
                for c in range(ROWS // CHUNK)
                for j in range(GROUP)
            ],
            0,
        )

    q_all = stacked(q_ref)
    g_all = stacked(g_ref)
    at = lax.broadcasted_iota(jnp.int32, (GROUP * ROWS, 1), 0)
    in_lead = (at // (GROUP * CHUNK)) * CHUNK + at % CHUNK < split
    zeros = jnp.zeros_like(q_all)
    q_pair = jnp.concatenate([jnp.where(in_lead, q_all, zeros), jnp.where(in_lead, zeros, q_all)], 1)
    g_pair = jnp.concatenate([jnp.where(in_lead, g_all, zeros), jnp.where(in_lead, zeros, g_all)], 1)
    dk_pair = dot(d_prompt[...], q_pair) * INV_SQRT
    dv_pair = dot(w_prompt[...], g_pair)
    for t in range(2):
        part_ref[:, t, 0] = dk_pair[:, t * HD : (t + 1) * HD].astype(BF16).reshape(16, 16, HD)
        part_ref[:, t, 1] = dv_pair[:, t * HD : (t + 1) * HD].astype(BF16).reshape(16, 16, HD)
    for chunk in range(ROWS // CHUNK):
        lo, hi = chunk * CHUNK, (chunk + 1) * CHUNK
        start = chunk * GROUP * CHUNK
        kg_ref[lo:hi] = (dot(d_local[lo:hi, start:], q_all[start:]) * INV_SQRT).astype(BF16)
        vg_ref[lo:hi] = dot(w_local[lo:hi, start:], g_all[start:]).astype(BF16)


def shards(query, comp_key, comp_value, prompt_key, prompt_value, out_grad, row_comp, prompt_owner):
    vmem = pl.BlockSpec(memory_space=pltpu.VMEM)
    smem = pl.BlockSpec(memory_space=pltpu.SMEM)
    dma = pltpu.SemaphoreType.DMA
    selected, slots = pl.pallas_call(
        gather_kernel,
        out_shape=(
            jax.ShapeDtypeStruct((PLANE, 2, 2, 16, COLS), BF16),
            jax.ShapeDtypeStruct((2 * PLANE,), jnp.int32),
        ),
        in_specs=[smem, smem, vmem, vmem],
        out_specs=(vmem, smem),
        scratch_shapes=[
            pltpu.VMEM((HEADS, 16, COLS), BF16),
            pltpu.VMEM((16, 16, COLS), BF16),
            pltpu.VMEM((NPROMPT, 2, 16, COLS), BF16),
            pltpu.VMEM((PLANE, 2, 2, 16, COLS), BF16),
            pltpu.VMEM((8, 128), jnp.int32),
            pltpu.VMEM((PLANE, 8, 128), jnp.int32),
            pltpu.SMEM((PLANE, 8, 128), jnp.int32),
            dma((16,)), dma((16,)), dma((16,)), dma((16,)), dma((16,)), dma((16,)), dma,
        ],
        compiler_params=pltpu.CompilerParams(collective_id=0, has_side_effects=True),
        name="gather",
    )(prompt_owner, row_comp, prompt_key, prompt_value)

    kv_local = COLS // HD
    wide = GROUP * HD
    attn_out, query_grad, key_grad, value_grad, parts = pl.pallas_call(
        attend_kernel,
        grid=(kv_local,),
        out_shape=(
            jax.ShapeDtypeStruct(query.shape, BF16),
            jax.ShapeDtypeStruct(query.shape, BF16),
            jax.ShapeDtypeStruct(comp_key.shape, BF16),
            jax.ShapeDtypeStruct(comp_key.shape, BF16),
            jax.ShapeDtypeStruct((PLANE, 2, 2, 16, COLS), BF16),
        ),
        in_specs=[
            pl.BlockSpec((4, 128), lambda g: (0, 0)),
            pl.BlockSpec((ROWS, wide), lambda g: (0, g)),
            pl.BlockSpec((ROWS, HD), lambda g: (0, g)),
            pl.BlockSpec((ROWS, HD), lambda g: (0, g)),
            pl.BlockSpec((PLANE, 2, 2, 16, HD), lambda g: (0, 0, 0, 0, g)),
            pl.BlockSpec((ROWS, wide), lambda g: (0, g)),
        ],
        out_specs=(
            pl.BlockSpec((ROWS, wide), lambda g: (0, g)),
            pl.BlockSpec((ROWS, wide), lambda g: (0, g)),
            pl.BlockSpec((ROWS, HD), lambda g: (0, g)),
            pl.BlockSpec((ROWS, HD), lambda g: (0, g)),
            pl.BlockSpec((PLANE, 2, 2, 16, HD), lambda g: (0, 0, 0, 0, g)),
        ),
        scratch_shapes=[
            pltpu.VMEM((PLEN, GROUP * ROWS), BF16),
            pltpu.VMEM((PLEN, GROUP * ROWS), BF16),
            pltpu.VMEM((ROWS, GROUP * ROWS), BF16),
            pltpu.VMEM((ROWS, GROUP * ROWS), BF16),
        ],
        compiler_params=pltpu.CompilerParams(vmem_limit_bytes=48 * 1024 * 1024),
        name="attend",
    )(row_comp.reshape(4, 128), query, comp_key, comp_value, selected, out_grad)

    prompt_key_grad, prompt_value_grad = pl.pallas_call(
        reduce_kernel,
        out_shape=(
            jax.ShapeDtypeStruct(prompt_key.shape, BF16),
            jax.ShapeDtypeStruct(prompt_key.shape, BF16),
        ),
        in_specs=[smem, vmem],
        out_specs=(vmem, vmem),
        scratch_shapes=[
            pltpu.VMEM((PLANE, 2, 2, 16, COLS), BF16),
            pltpu.VMEM((16, 16, COLS), BF16),
            pltpu.VMEM((16, 16, COLS), BF16),
            dma((16,)), dma((16,)), dma((16,)), dma((16,)),
        ],
        compiler_params=pltpu.CompilerParams(collective_id=1, has_side_effects=True),
        name="reduce",
    )(slots, parts)
    return (attn_out, query_grad, key_grad, value_grad, prompt_key_grad, prompt_value_grad)


def solution(mesh):
    placed = (
        P("seq", "head"),
        P("seq", "head"),
        P("seq", "head"),
        P(("seq", "head"), None),
        P(("seq", "head"), None),
        P("seq", "head"),
        P("seq"),
        P(),
    )
    return jax.shard_map(
        shards,
        mesh=mesh,
        in_specs=placed,
        out_specs=(
            P("seq", "head"),
            P("seq", "head"),
            P("seq", "head"),
            P("seq", "head"),
            P(("seq", "head"), None),
            P(("seq", "head"), None),
        ),
        check_vma=False,
    )
```

```python
import math

import jax
import jax.numpy as jnp
from jax import lax
from jax.experimental import pallas as pl
from jax.experimental.pallas import tpu as pltpu
from jax.sharding import PartitionSpec as P

QH = 32
KVH = 8
HD = 128
NPROMPT = 8
PLEN = 256
NGEN = 16
ROWS = 512
GROUP = QH // KVH
HEADS = 4
KV = 2
PLANE = 16
DEPTH = 4
CHUNK = 128
WIDE = GROUP * HD
SPAN = GROUP * CHUNK
CHUNKS = ROWS // CHUNK
MESH = pl.DeviceIdType.MESH
INV_SQRT = 1.0 / math.sqrt(HD)
EXP2_SCALE = INV_SQRT * math.log2(math.e)
NEG_FILL = -1e30
F32 = jnp.float32
BF16 = jnp.bfloat16


def place():
    seq = lax.axis_index("seq")
    head = lax.axis_index("head")
    return seq, head, seq // DEPTH, lax.rem(seq, DEPTH), seq // 8, 4 * lax.rem(seq, 8) + head


def spread_target(unit, i):
    return (unit // 2) * DEPTH + lax.rem(i, DEPTH), i // DEPTH


def holder_of(plane, i):
    unit = 2 * plane + lax.rem(i, 2)
    return 8 * (i // 2) + unit // 4, lax.rem(unit, 4)


def dot(a, b):
    return jnp.dot(a, b, preferred_element_type=F32)


def wait_bytes(ref, sem):
    pltpu.make_async_copy(ref, ref, sem).wait()


def kernel(
    owner_ref, comp_ref, q_hbm, k_hbm, v_hbm, pk_hbm, pv_hbm, g_hbm,
    out_hbm, qg_hbm, kg_hbm, vg_hbm, pkg_ref, pvg_ref,
    q_in, g_in, k_in, v_in, pk_in, pv_in,
    own_rows, dense, packed, picked, chosen_kv, info, infos, infos_smem,
    q_turn, g_turn, e_local, p_local, stats, w_prompt, d_prompt, w_local, d_local, o_turn, pair_turn,
    part, parts, pieces, finals, out_v, qg_v, kg_v, vg_v,
    in_sem, out_sem, local_sem, send_a, recv_a, send_i, recv_i, send_b, recv_b, send_c, recv_c, send_d, recv_d,
):
    seq, head, plane, z, slot, unit = place()
    barrier = pltpu.get_barrier_semaphore()

    def loop(lo, hi, body):
        def step(i, carry):
            body(i)
            return carry

        lax.fori_loop(lo, hi, step, 0)

    def peer(i):
        return lax.rem(plane + i, PLANE)

    def not_self(other, other_head):
        return jnp.logical_or(other != seq, other_head != head)

    def greet(i):
        for other, other_head in (spread_target(unit, i), holder_of(plane, i)):
            @pl.when(not_self(other, other_head))
            def _():
                pl.semaphore_signal(barrier, inc=1, device_id=(other, other_head), device_id_type=MESH)

    def greet_peer(i):
        pl.semaphore_signal(barrier, inc=1, device_id=(peer(i) * DEPTH + z, head), device_id_type=MESH)

    loop(0, 16, greet)
    loop(1, PLANE, greet_peer)

    loads = [
        pltpu.make_async_copy(pk_hbm, pk_in, in_sem.at[0]),
        pltpu.make_async_copy(pv_hbm, pv_in, in_sem.at[1]),
    ]
    for kv in range(KV):
        wide, narrow = pl.ds(kv * WIDE, WIDE), pl.ds(kv * HD, HD)
        for n, (src, dst, cols) in enumerate(
            ((q_hbm, q_in, wide), (k_hbm, k_in, narrow), (g_hbm, g_in, wide), (v_hbm, v_in, narrow))
        ):
            loads.append(pltpu.make_async_copy(src.at[:, cols], dst.at[kv], in_sem.at[2 + 4 * kv + n]))
    for load in loads:
        load.start()

    lead_comp = comp_ref[0]
    lead = owner_ref[lead_comp // NGEN]
    tail = owner_ref[comp_ref[ROWS - 1] // NGEN]
    split = jnp.int32(0)
    for step in (256, 128, 64, 32, 16, 8, 4, 2, 1):
        split = jnp.where(comp_ref[split + step - 1] == lead_comp, split + step, split)
    info[...] = jnp.where(lax.broadcasted_iota(jnp.int32, (8, 128), 0) < 4, lead, tail)
    infos[plane] = info[...]

    loads[0].wait()
    loads[1].wait()
    both = jnp.concatenate([pk_in[...].astype(F32), pv_in[...].astype(F32)], 0).astype(BF16)
    for other_head in range(HEADS):
        for kv in range(KV):
            lo = (KV * other_head + kv) * HD
            own_rows[other_head, kv] = both[:, lo : lo + HD]
    for load in loads[2:]:
        load.wait()

    lane_row = lax.broadcasted_iota(jnp.int32, (1, SPAN), 1) % CHUNK

    def before(kv):
        for chunk in range(CHUNKS):
            lo, hi = chunk * CHUNK, (chunk + 1) * CHUNK
            span = slice(chunk * SPAN, (chunk + 1) * SPAN)
            q_t = jnp.concatenate([q_in[kv, lo:hi, j * HD : (j + 1) * HD].T for j in range(GROUP)], 1)
            g_t = jnp.concatenate([g_in[kv, lo:hi, j * HD : (j + 1) * HD].T for j in range(GROUP)], 1)
            q_turn[kv, :, span] = q_t
            g_turn[kv, :, span] = g_t
            key_at = lax.broadcasted_iota(jnp.int32, (hi, CHUNK), 0)
            row_at = lo + lax.broadcasted_iota(jnp.int32, (hi, CHUNK), 1)
            seen = jnp.logical_and(key_at <= row_at, jnp.logical_or(key_at >= split, row_at < split))
            bias = jnp.where(seen, 0.0, NEG_FILL)
            scores = dot(k_in[kv, :hi], q_t) + jnp.concatenate([bias] * GROUP, 1)
            top = jnp.max(scores, axis=0, keepdims=True)
            raw = jnp.exp2((scores - top) * EXP2_SCALE)
            e_local[kv, :hi, span] = raw
            stats[kv, 0:1, span] = top
            stats[kv, 1:2, span] = jnp.sum(raw, axis=0, keepdims=True)
            p_local[kv, :hi, span] = dot(v_in[kv, :hi], g_t)

    def pair_of(turned, is_lead):
        zero = jnp.zeros_like(turned)
        return jnp.concatenate([jnp.where(is_lead, turned, zero), jnp.where(is_lead, zero, turned)], 0)

    def stacked(ref, kv):
        return jnp.concatenate(
            [
                ref[kv, c * CHUNK : (c + 1) * CHUNK, j * HD : (j + 1) * HD]
                for c in range(CHUNKS)
                for j in range(GROUP)
            ],
            0,
        )

    def stacked_pair(ref, kv):
        rows = stacked(ref, kv)
        at = lax.broadcasted_iota(jnp.int32, (GROUP * ROWS, 1), 0)
        in_lead = (at // SPAN) * CHUNK + at % CHUNK < split
        zero = jnp.zeros_like(rows)
        return jnp.concatenate([jnp.where(in_lead, rows, zero), jnp.where(in_lead, zero, rows)], 1)

    def middle(kv):
        key_pair = jnp.concatenate([chosen_kv[kv, :, t, 0].reshape(PLEN, HD) for t in range(2)], 1)
        value_pair = jnp.concatenate([chosen_kv[kv, :, t, 1].reshape(PLEN, HD) for t in range(2)], 1)
        pair_turn[kv] = key_pair.T
        value_pair_t = value_pair.T
        values_t = v_in[kv].T
        for chunk in range(CHUNKS):
            hi = (chunk + 1) * CHUNK
            span = slice(chunk * SPAN, (chunk + 1) * SPAN)
            is_lead = chunk * CHUNK + lane_row < split
            g_t = g_turn[kv, :, span]
            s_prompt = dot(key_pair, pair_of(q_turn[kv, :, span], is_lead))
            top_local = stats[kv, 0:1, span]
            top = jnp.maximum(top_local, jnp.max(s_prompt, axis=0, keepdims=True))
            e_prompt = jnp.exp2((s_prompt - top) * EXP2_SCALE)
            rescale = jnp.exp2((top_local - top) * EXP2_SCALE)
            inv = 1.0 / (jnp.sum(e_prompt, axis=0, keepdims=True) + rescale * stats[kv, 1:2, span])
            rescale = rescale * inv
            e_prompt = e_prompt * inv
            wh_prompt = e_prompt.astype(BF16)
            wh_local = (e_local[kv, :hi, span] * rescale).astype(BF16)
            w_prompt[kv, :, span] = wh_prompt
            w_local[kv, :hi, span] = wh_local
            o_pair = dot(value_pair_t, wh_prompt)
            o_t = jnp.where(is_lead, o_pair[:HD], o_pair[HD:]) + dot(values_t[:, :hi], wh_local)
            o_t = o_t.astype(BF16)
            o_turn[kv, :, span] = o_t
            delta = jnp.sum(o_t.astype(F32) * g_t.astype(F32), axis=0, keepdims=True)
            stats[kv, 2:3, span] = rescale
            stats[kv, 3:4, span] = delta
            d_prompt[kv, :, span] = (e_prompt * (dot(value_pair, pair_of(g_t, is_lead)) - delta)).astype(BF16)
        dk_pair = dot(d_prompt[kv], stacked_pair(q_in, kv)) * INV_SQRT
        dv_pair = dot(w_prompt[kv], stacked_pair(g_in, kv))
        for t in range(2):
            part[kv, :, t, 0] = dk_pair[:, t * HD : (t + 1) * HD].astype(BF16).reshape(PLANE, 16, HD)
            part[kv, :, t, 1] = dv_pair[:, t * HD : (t + 1) * HD].astype(BF16).reshape(PLANE, 16, HD)

    def after(kv):
        keys_t = k_in[kv].T
        for chunk in range(CHUNKS):
            lo, hi = chunk * CHUNK, (chunk + 1) * CHUNK
            span = slice(chunk * SPAN, (chunk + 1) * SPAN)
            is_lead = lo + lane_row < split
            rescale = stats[kv, 2:3, span]
            delta = stats[kv, 3:4, span]
            ds_local = ((e_local[kv, :hi, span] * rescale) * (p_local[kv, :hi, span] - delta)).astype(BF16)
            d_local[kv, :hi, span] = ds_local
            dq_pair = dot(pair_turn[kv], d_prompt[kv, :, span])
            dq_t = jnp.where(is_lead, dq_pair[:HD], dq_pair[HD:]) + dot(keys_t[:, :hi], ds_local)
            dq_t = (dq_t * INV_SQRT).astype(BF16)
            o_t = o_turn[kv, :, span]
            for j in range(GROUP):
                cols = slice(j * HD, (j + 1) * HD)
                out_v[kv, lo:hi, cols] = o_t[:, j * CHUNK : (j + 1) * CHUNK].T
                qg_v[kv, lo:hi, cols] = dq_t[:, j * CHUNK : (j + 1) * CHUNK].T
        q_all = stacked(q_in, kv)
        g_all = stacked(g_in, kv)
        for chunk in range(CHUNKS):
            lo, hi = chunk * CHUNK, (chunk + 1) * CHUNK
            start = chunk * SPAN
            kg_v[kv, lo:hi] = (dot(d_local[kv, lo:hi, start:], q_all[start:]) * INV_SQRT).astype(BF16)
            vg_v[kv, lo:hi] = dot(w_local[kv, lo:hi, start:], g_all[start:]).astype(BF16)

    def store(kv, n, src, dst, width):
        cols = pl.ds(pl.multiple_of(kv * width, width), width)
        return pltpu.make_async_copy(src.at[kv], dst.at[:, cols], out_sem.at[4 * kv + n])

    def stores(kv):
        return (
            store(kv, 0, out_v, out_hbm, WIDE), store(kv, 1, qg_v, qg_hbm, WIDE),
            store(kv, 2, kg_v, kg_hbm, HD), store(kv, 3, vg_v, vg_hbm, HD),
        )

    def copy_a(i):
        other, other_head = spread_target(unit, i)
        at = 2 * slot + lax.rem(unit, 2)
        return not_self(other, other_head), pltpu.make_async_remote_copy(
            src_ref=own_rows.at[i // DEPTH], dst_ref=dense.at[at], send_sem=send_a.at[i], recv_sem=recv_a.at[at],
            device_id=(other, other_head), device_id_type=MESH,
        )

    def start_a(i):
        away, copy = copy_a(i)

        @pl.when(jnp.logical_not(away))
        def _():
            at = 2 * slot + lax.rem(unit, 2)
            pltpu.make_async_copy(own_rows.at[i // DEPTH], dense.at[at], recv_a.at[at]).start()

        @pl.when(away)
        def _():
            copy.start()

    def copy_info(i):
        return pltpu.make_async_remote_copy(
            src_ref=info, dst_ref=infos.at[plane], send_sem=send_i.at[i], recv_sem=recv_i.at[plane],
            device_id=(peer(i) * DEPTH + z, head), device_id_type=MESH,
        )

    def copy_b(kv, i):
        return pltpu.make_async_remote_copy(
            src_ref=picked.at[kv, i], dst_ref=chosen_kv.at[kv, plane],
            send_sem=send_b.at[kv, i], recv_sem=recv_b.at[kv, plane],
            device_id=(peer(i) * DEPTH + z, head), device_id_type=MESH,
        )

    def copy_c(kv, i):
        return pltpu.make_async_remote_copy(
            src_ref=part.at[kv, peer(i)], dst_ref=parts.at[kv, plane],
            send_sem=send_c.at[kv, i], recv_sem=recv_c.at[kv, plane],
            device_id=(peer(i) * DEPTH + z, head), device_id_type=MESH,
        )

    def copy_d(i):
        other, other_head = holder_of(plane, i)
        at = DEPTH * head + z
        return not_self(other, other_head), pltpu.make_async_remote_copy(
            src_ref=pieces.at[i], dst_ref=finals.at[at], send_sem=send_d.at[i], recv_sem=recv_d.at[at],
            device_id=(other, other_head), device_id_type=MESH,
        )

    def start_d(i):
        away, copy = copy_d(i)

        @pl.when(jnp.logical_not(away))
        def _():
            at = DEPTH * head + z
            pltpu.make_async_copy(pieces.at[i], finals.at[at], recv_d.at[at]).start()

        @pl.when(away)
        def _():
            copy.start()

    before(0)
    own = unit // 2 == plane

    @pl.when(own)
    def _():
        pl.semaphore_wait(barrier, 15 + 30)

    @pl.when(jnp.logical_not(own))
    def _():
        pl.semaphore_wait(barrier, 15 + 32)

    loop(0, 16, start_a)
    loop(1, PLANE, lambda i: copy_info(i).start())
    before(1)
    loop(1, PLANE, lambda i: wait_bytes(infos.at[peer(i)], recv_i.at[peer(i)]))
    to_smem = pltpu.make_async_copy(infos, infos_smem, local_sem)
    to_smem.start()
    loop(0, 16, lambda i: wait_bytes(dense.at[i], recv_a.at[i]))
    to_smem.wait()
    for p in range(NPROMPT):
        for kv in range(KV):
            first = dense[2 * p, kv].astype(F32)
            second = dense[2 * p + 1, kv].astype(F32)
            packed[kv, p, 0] = jnp.concatenate([first[:8], second[:8]], 0).astype(BF16)
            packed[kv, p, 1] = jnp.concatenate([first[8:], second[8:]], 0).astype(BF16)

    for kv in range(KV):
        def start_b(i):
            picked[kv, i, 0] = packed[kv, infos_smem[peer(i), 0, 0]]
            picked[kv, i, 1] = packed[kv, infos_smem[peer(i), 4, 0]]
            copy_b(kv, i).start()

        loop(1, PLANE, start_b)
        chosen_kv[kv, plane, 0] = packed[kv, lead]
        chosen_kv[kv, plane, 1] = packed[kv, tail]

    def middle_step(kv):
        loop(1, PLANE, lambda i: wait_bytes(chosen_kv.at[kv, peer(i)], recv_b.at[kv, peer(i)]))
        middle(kv)
        loop(1, PLANE, lambda i: copy_c(kv, i).start())
        parts[kv, plane] = part[kv, plane]

    loop(0, KV, middle_step)

    terms = 2 * PLANE * 16
    lane = lax.broadcasted_iota(jnp.int32, (1, terms), 1)
    lane_slot = jnp.zeros((1, terms), jnp.int32)
    for i in range(PLANE):
        lane_slot = jnp.where(lane // 16 == 2 * i, infos_smem[i, 0, 0], lane_slot)
        lane_slot = jnp.where(lane // 16 == 2 * i + 1, infos_smem[i, 4, 0], lane_slot)
    row = lax.broadcasted_iota(jnp.int32, (NPROMPT * 16, terms), 0)
    lanes = lax.broadcasted_iota(jnp.int32, (NPROMPT * 16, terms), 1)
    chosen = jnp.logical_and(row // 16 == lane_slot, lax.rem(row, 16) == lax.rem(lanes, 16))
    chosen = jnp.where(chosen, 1.0, 0.0).astype(BF16)

    def after_step(kv):
        after(kv)
        for copy in stores(kv):
            copy.start()

    loop(0, KV, after_step)

    for kv in range(KV):
        loop(1, PLANE, lambda i: wait_bytes(parts.at[kv, peer(i)], recv_c.at[kv, peer(i)]))
        sums = [dot(chosen, parts[kv, :, :, n].reshape(terms, HD)) for n in range(2)]
        for i in range(2 * NPROMPT):
            lo = 8 * i
            pieces[i, kv] = jnp.concatenate([sums[0][lo : lo + 8], sums[1][lo : lo + 8]], 0).astype(BF16)
    loop(0, 16, start_d)

    def wait_sends(i):
        copy_info(i).wait_send()
        for kv in range(KV):
            copy_b(kv, i).wait_send()
            copy_c(kv, i).wait_send()

    def wait_send_a(i):
        away, copy = copy_a(i)

        @pl.when(away)
        def _():
            copy.wait_send()

    def wait_send_d(i):
        away, copy = copy_d(i)

        @pl.when(away)
        def _():
            copy.wait_send()

    loop(1, PLANE, wait_sends)
    loop(0, 16, wait_send_a)
    for kv in range(KV):
        for copy in stores(kv):
            copy.wait()
    loop(0, 16, lambda i: wait_bytes(finals.at[i], recv_d.at[i]))
    for other_head in range(HEADS):
        for kv in range(KV):
            total = finals[DEPTH * other_head, kv].astype(F32)
            for other_z in range(1, DEPTH):
                total = total + finals[DEPTH * other_head + other_z, kv].astype(F32)
            lo = (KV * other_head + kv) * HD
            pkg_ref[:, lo : lo + HD] = total[:8].astype(BF16)
            pvg_ref[:, lo : lo + HD] = total[8:].astype(BF16)
    loop(0, 16, wait_send_d)


def shards(query, comp_key, comp_value, prompt_key, prompt_value, out_grad, row_comp, prompt_owner):
    vmem = pl.BlockSpec(memory_space=pltpu.VMEM)
    smem = pl.BlockSpec(memory_space=pltpu.SMEM)
    hbm = pl.BlockSpec(memory_space=pl.ANY)
    dma = pltpu.SemaphoreType.DMA
    wide_rows = (KV, ROWS, WIDE)
    rows = (KV, ROWS, HD)
    heads_wide = GROUP * ROWS
    prompt_rows = prompt_key.shape
    like = lambda a: jax.ShapeDtypeStruct(a.shape, BF16)
    buf = pltpu.VMEM
    return pl.pallas_call(
        kernel,
        out_shape=(
            like(query), like(query), like(comp_key), like(comp_value), like(prompt_key), like(prompt_value),
        ),
        in_specs=[smem, smem] + [hbm] * 6,
        out_specs=(hbm, hbm, hbm, hbm, vmem, vmem),
        scratch_shapes=[
            buf(wide_rows, BF16), buf(wide_rows, BF16), buf(rows, BF16), buf(rows, BF16),
            buf(prompt_rows, BF16), buf(prompt_rows, BF16),
            buf((HEADS, KV, 16, HD), BF16),
            buf((16, KV, 16, HD), BF16),
            buf((KV, NPROMPT, 2, 16, HD), BF16),
            buf((KV, PLANE, 2, 2, 16, HD), BF16),
            buf((KV, PLANE, 2, 2, 16, HD), BF16),
            buf((8, 128), jnp.int32),
            buf((PLANE, 8, 128), jnp.int32),
            pltpu.SMEM((PLANE, 8, 128), jnp.int32),
            buf((KV, HD, heads_wide), BF16),
            buf((KV, HD, heads_wide), BF16),
            buf((KV, ROWS, heads_wide), F32),
            buf((KV, ROWS, heads_wide), F32),
            buf((KV, 8, heads_wide), F32),
            buf((KV, PLEN, heads_wide), BF16),
            buf((KV, PLEN, heads_wide), BF16),
            buf((KV, ROWS, heads_wide), BF16),
            buf((KV, ROWS, heads_wide), BF16),
            buf((KV, HD, heads_wide), BF16),
            buf((KV, 2 * HD, PLEN), BF16),
            buf((KV, PLANE, 2, 2, 16, HD), BF16),
            buf((KV, PLANE, 2, 2, 16, HD), BF16),
            buf((16, KV, 16, HD), BF16),
            buf((16, KV, 16, HD), BF16),
            buf(wide_rows, BF16), buf(wide_rows, BF16), buf(rows, BF16), buf(rows, BF16),
            dma((10,)), dma((8,)), dma,
            dma((16,)), dma((16,)), dma((PLANE,)), dma((PLANE,)),
            dma((KV, PLANE)), dma((KV, PLANE)), dma((KV, PLANE)), dma((KV, PLANE)),
            dma((16,)), dma((16,)),
        ],
        compiler_params=pltpu.CompilerParams(
            collective_id=0, has_side_effects=True, vmem_limit_bytes=56 * 1024 * 1024
        ),
        name="attend",
    )(prompt_owner, row_comp, query, comp_key, comp_value, prompt_key, prompt_value, out_grad)


def solution(mesh):
    placed = (
        P("seq", "head"),
        P("seq", "head"),
        P("seq", "head"),
        P(("seq", "head"), None),
        P(("seq", "head"), None),
        P("seq", "head"),
        P("seq"),
        P(),
    )
    return jax.shard_map(
        shards,
        mesh=mesh,
        in_specs=placed,
        out_specs=(
            P("seq", "head"),
            P("seq", "head"),
            P("seq", "head"),
            P("seq", "head"),
            P(("seq", "head"), None),
            P(("seq", "head"), None),
        ),
        check_vma=False,
    )
```

```python
import math

import jax
import jax.numpy as jnp
from jax import lax
from jax.experimental import pallas as pl
from jax.experimental.pallas import tpu as pltpu
from jax.sharding import PartitionSpec as P

QH = 32
KVH = 8
HD = 128
NPROMPT = 8
PLEN = 256
NGEN = 16
ROWS = 512
GROUP = QH // KVH
HEADS = 4
KV = 2
PLANE = 16
DEPTH = 4
CHUNK = 128
WIDE = GROUP * HD
SPAN = GROUP * CHUNK
CHUNKS = ROWS // CHUNK
MESH = pl.DeviceIdType.MESH
INV_SQRT = 1.0 / math.sqrt(HD)
EXP2_SCALE = INV_SQRT * math.log2(math.e)
NEG_FILL = -1e30
F32 = jnp.float32
BF16 = jnp.bfloat16


def place():
    seq = lax.axis_index("seq")
    head = lax.axis_index("head")
    x, y, z = seq // 16, lax.rem(seq // 4, 4), lax.rem(seq, 4)
    return seq, head, x, y, z, 2 * z + head // 2, lax.rem(head, 2), seq // 8


FAR_Z = (2, 1, 3, 0)
FAR_Z8 = (4, 3, 5, 2, 6, 1, 7, 0)
FAR_XY = sorted(
    ((dx, dy) for dx in range(4) for dy in range(4) if (dx, dy) != (0, 0)),
    key=lambda d: -(min(d[0], 4 - d[0]) + min(d[1], 4 - d[1])),
)


def dot(a, b):
    return jnp.dot(a, b, preferred_element_type=F32)


def wait_bytes(ref, sem):
    pltpu.make_async_copy(ref, ref, sem).wait()


def kernel(
    owner_hbm, comp_hbm, q_hbm, k_hbm, v_hbm, pk_hbm, pv_hbm, g_hbm,
    out_hbm, qg_hbm, kg_hbm, vg_hbm, pkg_ref, pvg_ref,
    owner_ref, comp_ref, q_in, g_in, k_in, v_in, pk_in, pv_in,
    own_rows, dense, packed, picked, chosen_kv, info, infos, infos_smem,
    q_turn, g_turn, e_local, p_local, o_local, stats, w_prompt, d_prompt, w_local, d_local, o_turn, pair_turn,
    part, parts, pieces, finals, out_v, qg_v, kg_v, vg_v,
    in_sem, out_sem, local_sem, send_a, recv_a, send_i, recv_i, send_b, recv_b, send_c, recv_c, send_d, recv_d,
):
    seq, head, x, y, z, z8, core, slot = place()
    plane = 4 * x + y
    barrier = pltpu.get_barrier_semaphore()

    served = lax.rem(z8 - slot + 8, 8)
    column = 4 * (served // 2) + 2 * lax.rem(served, 2) + lax.rem(y, 2)
    own = column == plane
    self_slot = lax.rem(z8 - slot + 8, 8) == slot

    def spread_target(dz, other_head):
        return column * DEPTH + lax.rem(z + dz, DEPTH), jnp.int32(other_head)

    def holder(off, k):
        other_slot = lax.rem(z8 + off - slot + 8, 8)
        other_z8 = lax.rem(z8 + off, 8)
        other_y = 2 * lax.rem(other_slot, 2) + lax.rem(y, 2)
        other = 16 * (other_slot // 2) + 4 * other_y + other_z8 // 2
        return other_slot, other, 2 * lax.rem(other_z8, 2) + k

    def xy_peer(d):
        return 4 * lax.rem(x + d[0], 4) + lax.rem(y + d[1], 4)

    def signal(other, other_head):
        pl.semaphore_signal(barrier, inc=1, device_id=(other, other_head), device_id_type=MESH)

    def greet_spread(dz):
        for other_head in range(HEADS):
            other, _ = spread_target(dz, other_head)
            if dz:
                signal(other, jnp.int32(other_head))
            else:
                @pl.when(jnp.logical_not(jnp.logical_and(own, head == other_head)))
                def _():
                    signal(other, jnp.int32(other_head))

    def greet_holder(off):
        for k in range(2):
            _, other, other_head = holder(off, k)
            if off:
                signal(other, other_head)
            else:
                @pl.when(jnp.logical_not(jnp.logical_and(self_slot, core == k)))
                def _():
                    signal(other, other_head)

    greet_spread(2)
    for off in (4, 3, 5):
        greet_holder(off)
    greet_spread(1)
    greet_spread(3)
    for off in (2, 6):
        greet_holder(off)
    greet_spread(0)
    for off in (1, 7, 0):
        greet_holder(off)
    for d in FAR_XY:
        signal(xy_peer(d) * DEPTH + z, head)

    loads = [
        pltpu.make_async_copy(pk_hbm, pk_in, in_sem.at[0]),
        pltpu.make_async_copy(pv_hbm, pv_in, in_sem.at[1]),
        pltpu.make_async_copy(owner_hbm, owner_ref, in_sem.at[10]),
        pltpu.make_async_copy(comp_hbm, comp_ref, in_sem.at[11]),
    ]
    for kv in range(KV):
        wide, narrow = pl.ds(kv * WIDE, WIDE), pl.ds(kv * HD, HD)
        for n, (src, dst, cols) in enumerate(
            ((q_hbm, q_in, wide), (k_hbm, k_in, narrow), (g_hbm, g_in, wide), (v_hbm, v_in, narrow))
        ):
            loads.append(pltpu.make_async_copy(src.at[:, cols], dst.at[kv], in_sem.at[2 + 4 * kv + n]))
    for load in loads:
        load.start()
    for load in loads[:4]:
        load.wait()

    both = jnp.concatenate([pk_in[...].astype(F32), pv_in[...].astype(F32)], 0).astype(BF16)
    for other_head in range(HEADS):
        for kv in range(KV):
            lo = (KV * other_head + kv) * HD
            own_rows[other_head, kv] = both[:, lo : lo + HD]

    lead_comp = comp_ref[0]
    lead = owner_ref[lead_comp // NGEN]
    tail = owner_ref[comp_ref[ROWS - 1] // NGEN]
    split = jnp.int32(0)
    for step in (256, 128, 64, 32, 16, 8, 4, 2, 1):
        split = jnp.where(comp_ref[split + step - 1] == lead_comp, split + step, split)
    info[...] = jnp.where(lax.broadcasted_iota(jnp.int32, (8, 128), 0) < 4, lead, tail)
    infos[plane] = info[...]

    for load in loads[4:]:
        load.wait()

    def loop(lo, hi, body):
        def step(i, carry):
            body(i)
            return carry

        lax.fori_loop(lo, hi, step, 0)

    lane_row = lax.broadcasted_iota(jnp.int32, (1, SPAN), 1) % CHUNK

    def before(kv):
        values_t = v_in[kv].T
        for chunk in range(CHUNKS):
            lo, hi = chunk * CHUNK, (chunk + 1) * CHUNK
            span = slice(chunk * SPAN, (chunk + 1) * SPAN)
            q_t = jnp.concatenate([q_in[kv, lo:hi, j * HD : (j + 1) * HD].T for j in range(GROUP)], 1)
            g_t = jnp.concatenate([g_in[kv, lo:hi, j * HD : (j + 1) * HD].T for j in range(GROUP)], 1)
            q_turn[kv, :, span] = q_t
            g_turn[kv, :, span] = g_t
            key_at = lax.broadcasted_iota(jnp.int32, (hi, CHUNK), 0)
            row_at = lo + lax.broadcasted_iota(jnp.int32, (hi, CHUNK), 1)
            seen = jnp.logical_and(key_at <= row_at, jnp.logical_or(key_at >= split, row_at < split))
            bias = jnp.where(seen, 0.0, NEG_FILL)
            scores = dot(k_in[kv, :hi], q_t) + jnp.concatenate([bias] * GROUP, 1)
            top = jnp.max(scores, axis=0, keepdims=True)
            raw = jnp.exp2((scores - top) * EXP2_SCALE)
            e_local[kv, :hi, span] = raw
            o_local[kv, :, span] = dot(values_t[:, :hi], raw.astype(BF16))
            stats[kv, 0:1, span] = top
            stats[kv, 1:2, span] = jnp.sum(raw, axis=0, keepdims=True)
            p_local[kv, :hi, span] = dot(v_in[kv, :hi], g_t)

    def pair_of(turned, is_lead):
        zero = jnp.zeros_like(turned)
        return jnp.concatenate([jnp.where(is_lead, turned, zero), jnp.where(is_lead, zero, turned)], 0)

    def stacked(ref, kv):
        return jnp.concatenate(
            [
                ref[kv, c * CHUNK : (c + 1) * CHUNK, j * HD : (j + 1) * HD]
                for c in range(CHUNKS)
                for j in range(GROUP)
            ],
            0,
        )

    def stacked_pair(ref, kv):
        rows = stacked(ref, kv)
        at = lax.broadcasted_iota(jnp.int32, (GROUP * ROWS, 1), 0)
        in_lead = (at // SPAN) * CHUNK + at % CHUNK < split
        zero = jnp.zeros_like(rows)
        return jnp.concatenate([jnp.where(in_lead, rows, zero), jnp.where(in_lead, zero, rows)], 1)

    def middle(kv):
        key_pair = jnp.concatenate([chosen_kv[:, kv, t, 0].reshape(PLEN, HD) for t in range(2)], 1)
        value_pair = jnp.concatenate([chosen_kv[:, kv, t, 1].reshape(PLEN, HD) for t in range(2)], 1)
        pair_turn[kv] = key_pair.T
        value_pair_t = value_pair.T
        for chunk in range(CHUNKS):
            span = slice(chunk * SPAN, (chunk + 1) * SPAN)
            is_lead = chunk * CHUNK + lane_row < split
            g_t = g_turn[kv, :, span]
            s_prompt = dot(key_pair, pair_of(q_turn[kv, :, span], is_lead))
            top_local = stats[kv, 0:1, span]
            top = jnp.maximum(top_local, jnp.max(s_prompt, axis=0, keepdims=True))
            e_prompt = jnp.exp2((s_prompt - top) * EXP2_SCALE)
            rescale = jnp.exp2((top_local - top) * EXP2_SCALE)
            inv = 1.0 / (jnp.sum(e_prompt, axis=0, keepdims=True) + rescale * stats[kv, 1:2, span])
            rescale = rescale * inv
            e_prompt = e_prompt * inv
            wh_prompt = e_prompt.astype(BF16)
            w_prompt[kv, :, span] = wh_prompt
            o_pair = dot(value_pair_t, wh_prompt)
            o_t = jnp.where(is_lead, o_pair[:HD], o_pair[HD:]) + o_local[kv, :, span] * rescale
            o_t = o_t.astype(BF16)
            o_turn[kv, :, span] = o_t
            delta = jnp.sum(o_t.astype(F32) * g_t.astype(F32), axis=0, keepdims=True)
            stats[kv, 2:3, span] = rescale
            stats[kv, 3:4, span] = delta
            d_prompt[kv, :, span] = (e_prompt * (dot(value_pair, pair_of(g_t, is_lead)) - delta)).astype(BF16)
        dk_pair = dot(d_prompt[kv], stacked_pair(q_in, kv)) * INV_SQRT
        dv_pair = dot(w_prompt[kv], stacked_pair(g_in, kv))
        for t in range(2):
            part[kv, :, t, 0] = dk_pair[:, t * HD : (t + 1) * HD].astype(BF16).reshape(PLANE, 16, HD)
            part[kv, :, t, 1] = dv_pair[:, t * HD : (t + 1) * HD].astype(BF16).reshape(PLANE, 16, HD)

    def after(kv):
        keys_t = k_in[kv].T
        for chunk in range(CHUNKS):
            lo, hi = chunk * CHUNK, (chunk + 1) * CHUNK
            span = slice(chunk * SPAN, (chunk + 1) * SPAN)
            is_lead = lo + lane_row < split
            rescale = stats[kv, 2:3, span]
            delta = stats[kv, 3:4, span]
            weights = e_local[kv, :hi, span] * rescale
            w_local[kv, :hi, span] = weights.astype(BF16)
            ds_local = (weights * (p_local[kv, :hi, span] - delta)).astype(BF16)
            d_local[kv, :hi, span] = ds_local
            dq_pair = dot(pair_turn[kv], d_prompt[kv, :, span])
            dq_t = jnp.where(is_lead, dq_pair[:HD], dq_pair[HD:]) + dot(keys_t[:, :hi], ds_local)
            dq_t = (dq_t * INV_SQRT).astype(BF16)
            o_t = o_turn[kv, :, span]
            for j in range(GROUP):
                cols = slice(j * HD, (j + 1) * HD)
                out_v[kv, lo:hi, cols] = o_t[:, j * CHUNK : (j + 1) * CHUNK].T
                qg_v[kv, lo:hi, cols] = dq_t[:, j * CHUNK : (j + 1) * CHUNK].T
        q_all = stacked(q_in, kv)
        g_all = stacked(g_in, kv)
        for chunk in range(CHUNKS):
            lo, hi = chunk * CHUNK, (chunk + 1) * CHUNK
            start = chunk * SPAN
            kg_v[kv, lo:hi] = (dot(d_local[kv, lo:hi, start:], q_all[start:]) * INV_SQRT).astype(BF16)
            vg_v[kv, lo:hi] = dot(w_local[kv, lo:hi, start:], g_all[start:]).astype(BF16)

    def store(kv, n, src, dst, width):
        cols = pl.ds(pl.multiple_of(kv * width, width), width)
        return pltpu.make_async_copy(src.at[kv], dst.at[:, cols], out_sem.at[4 * kv + n])

    def stores(kv):
        return (
            store(kv, 0, out_v, out_hbm, WIDE), store(kv, 1, qg_v, qg_hbm, WIDE),
            store(kv, 2, kg_v, kg_hbm, HD), store(kv, 3, vg_v, vg_hbm, HD),
        )

    def copy_a(dz, other_head):
        at = 2 * slot + core
        return pltpu.make_async_remote_copy(
            src_ref=own_rows.at[other_head], dst_ref=dense.at[at],
            send_sem=send_a.at[4 * dz + other_head], recv_sem=recv_a.at[at],
            device_id=spread_target(dz, other_head), device_id_type=MESH,
        )

    def self_a(other_head):
        return jnp.logical_and(own, head == other_head)

    def start_a(dz, other_head):
        if dz:
            copy_a(dz, other_head).start()
            return
        at = 2 * slot + core

        @pl.when(self_a(other_head))
        def _():
            pltpu.make_async_copy(own_rows.at[other_head], dense.at[at], recv_a.at[at]).start()

        @pl.when(jnp.logical_not(self_a(other_head)))
        def _():
            copy_a(dz, other_head).start()

    def wait_send_a(dz, other_head):
        if dz:
            copy_a(dz, other_head).wait_send()
            return

        @pl.when(jnp.logical_not(self_a(other_head)))
        def _():
            copy_a(dz, other_head).wait_send()

    def copy_info(n):
        return pltpu.make_async_remote_copy(
            src_ref=info, dst_ref=infos.at[plane], send_sem=send_i.at[n], recv_sem=recv_i.at[plane],
            device_id=(xy_peer(FAR_XY[n]) * DEPTH + z, head), device_id_type=MESH,
        )

    def copy_b(n):
        return pltpu.make_async_remote_copy(
            src_ref=picked.at[n], dst_ref=chosen_kv.at[plane], send_sem=send_b.at[n], recv_sem=recv_b.at[plane],
            device_id=(xy_peer(FAR_XY[n]) * DEPTH + z, head), device_id_type=MESH,
        )

    def copy_c(kv, n):
        other = xy_peer(FAR_XY[n])
        return pltpu.make_async_remote_copy(
            src_ref=part.at[kv, other], dst_ref=parts.at[kv, plane],
            send_sem=send_c.at[kv, n], recv_sem=recv_c.at[kv, plane],
            device_id=(other * DEPTH + z, head), device_id_type=MESH,
        )

    def copy_d(off, k):
        other_slot, other, other_head = holder(off, k)
        at = DEPTH * head + z
        return other_slot, pltpu.make_async_remote_copy(
            src_ref=pieces.at[2 * other_slot + k], dst_ref=finals.at[at],
            send_sem=send_d.at[2 * off + k], recv_sem=recv_d.at[at],
            device_id=(other, other_head), device_id_type=MESH,
        )

    def self_d(k):
        return jnp.logical_and(self_slot, core == k)

    def start_d(off, k):
        other_slot, copy = copy_d(off, k)
        if off:
            copy.start()
            return
        at = DEPTH * head + z

        @pl.when(self_d(k))
        def _():
            pltpu.make_async_copy(pieces.at[2 * other_slot + k], finals.at[at], recv_d.at[at]).start()

        @pl.when(jnp.logical_not(self_d(k)))
        def _():
            copy.start()

    def wait_send_d(off, k):
        _, copy = copy_d(off, k)
        if off:
            copy.wait_send()
            return

        @pl.when(jnp.logical_not(self_d(k)))
        def _():
            copy.wait_send()

    before(0)

    @pl.when(own)
    def _():
        pl.semaphore_wait(barrier, 15 + 15 + 15)

    @pl.when(jnp.logical_not(own))
    def _():
        pl.semaphore_wait(barrier, 15 + 16 + 16)

    for dz in FAR_Z:
        for other_head in range(HEADS):
            start_a(dz, other_head)
    for n in range(PLANE - 1):
        copy_info(n).start()
    before(1)
    for d in FAR_XY:
        other = xy_peer(d)
        wait_bytes(infos.at[other], recv_i.at[other])
    to_smem = pltpu.make_async_copy(infos, infos_smem, local_sem)
    to_smem.start()
    loop(0, 16, lambda i: wait_bytes(dense.at[i], recv_a.at[i]))
    to_smem.wait()
    for p in range(NPROMPT):
        for kv in range(KV):
            first = dense[2 * p, kv].astype(F32)
            second = dense[2 * p + 1, kv].astype(F32)
            packed[p, kv, 0] = jnp.concatenate([first[:8], second[:8]], 0).astype(BF16)
            packed[p, kv, 1] = jnp.concatenate([first[8:], second[8:]], 0).astype(BF16)
    for n, d in enumerate(FAR_XY):
        other = xy_peer(d)
        other_lead = infos_smem[other, 0, 0]
        other_tail = infos_smem[other, 4, 0]
        for kv in range(KV):
            picked[n, kv, 0] = packed[other_lead, kv]
            picked[n, kv, 1] = packed[other_tail, kv]
        copy_b(n).start()
    for kv in range(KV):
        chosen_kv[plane, kv, 0] = packed[lead, kv]
        chosen_kv[plane, kv, 1] = packed[tail, kv]
    for d in FAR_XY:
        other = xy_peer(d)
        wait_bytes(chosen_kv.at[other], recv_b.at[other])

    def middle_step(kv):
        middle(kv)
        for n in range(PLANE - 1):
            copy_c(kv, n).start()
        parts[kv, plane] = part[kv, plane]

    loop(0, KV, middle_step)

    terms = 2 * PLANE * 16
    lane = lax.broadcasted_iota(jnp.int32, (1, terms), 1)
    lane_slot = jnp.zeros((1, terms), jnp.int32)
    for i in range(PLANE):
        lane_slot = jnp.where(lane // 16 == 2 * i, infos_smem[i, 0, 0], lane_slot)
        lane_slot = jnp.where(lane // 16 == 2 * i + 1, infos_smem[i, 4, 0], lane_slot)
    row = lax.broadcasted_iota(jnp.int32, (NPROMPT * 16, terms), 0)
    lanes = lax.broadcasted_iota(jnp.int32, (NPROMPT * 16, terms), 1)
    chosen = jnp.logical_and(row // 16 == lane_slot, lax.rem(row, 16) == lax.rem(lanes, 16))
    chosen = jnp.where(chosen, 1.0, 0.0).astype(BF16)

    def after_step(kv):
        after(kv)
        for copy in stores(kv):
            copy.start()

    loop(0, KV, after_step)

    for kv in range(KV):
        for d in FAR_XY:
            other = xy_peer(d)
            wait_bytes(parts.at[kv, other], recv_c.at[kv, other])
        sums = [dot(chosen, parts[kv, :, :, n].reshape(terms, HD)) for n in range(2)]
        for i in range(2 * NPROMPT):
            lo = 8 * i
            pieces[i, kv] = jnp.concatenate([sums[0][lo : lo + 8], sums[1][lo : lo + 8]], 0).astype(BF16)
    for off in FAR_Z8:
        for k in range(2):
            start_d(off, k)

    for n in range(PLANE - 1):
        copy_info(n).wait_send()
        copy_b(n).wait_send()
        for kv in range(KV):
            copy_c(kv, n).wait_send()
    for dz in FAR_Z:
        for other_head in range(HEADS):
            wait_send_a(dz, other_head)
    for kv in range(KV):
        for copy in stores(kv):
            copy.wait()
    loop(0, 16, lambda i: wait_bytes(finals.at[i], recv_d.at[i]))
    for other_head in range(HEADS):
        for kv in range(KV):
            total = finals[DEPTH * other_head, kv].astype(F32)
            for other_z in range(1, DEPTH):
                total = total + finals[DEPTH * other_head + other_z, kv].astype(F32)
            lo = (KV * other_head + kv) * HD
            pkg_ref[:, lo : lo + HD] = total[:8].astype(BF16)
            pvg_ref[:, lo : lo + HD] = total[8:].astype(BF16)
    for off in FAR_Z8:
        for k in range(2):
            wait_send_d(off, k)


def hand_over(*refs):
    sources, targets, held, sem_in, sem_out = refs[:6], refs[6:12], refs[12:18], refs[18], refs[19]
    loads, stores = [], []
    for src, dst, mid in zip(sources, targets, held):
        step = src.shape[0] // 4 if src.shape[0] >= 64 else src.shape[0]
        for lo in range(0, src.shape[0], step):
            rows = pl.ds(lo, step)
            n = len(loads)
            loads.append(pltpu.make_async_copy(src.at[rows], mid.at[rows], sem_in.at[n]))
            stores.append(pltpu.make_async_copy(mid.at[rows], dst.at[rows], sem_out.at[n]))
    for load in loads:
        load.start()
    for load, store in zip(loads, stores):
        load.wait()
        store.start()
    for store in stores:
        store.wait()


def shards(query, comp_key, comp_value, prompt_key, prompt_value, out_grad, row_comp, prompt_owner):
    vmem = pl.BlockSpec(memory_space=pltpu.VMEM)
    smem = pl.BlockSpec(memory_space=pltpu.SMEM)
    hbm = pl.BlockSpec(memory_space=pl.ANY)
    dma = pltpu.SemaphoreType.DMA
    wide_rows = (KV, ROWS, WIDE)
    rows = (KV, ROWS, HD)
    heads_wide = GROUP * ROWS
    prompt_rows = prompt_key.shape
    like = lambda a: jax.ShapeDtypeStruct(a.shape, BF16)
    buf = pltpu.VMEM
    results = pl.pallas_call(
        kernel,
        out_shape=(
            like(query), like(query), like(comp_key), like(comp_value), like(prompt_key), like(prompt_value),
        ),
        in_specs=[hbm] * 8,
        out_specs=(hbm, hbm, hbm, hbm, vmem, vmem),
        scratch_shapes=[
            pltpu.SMEM((NPROMPT,), jnp.int32), pltpu.SMEM((ROWS,), jnp.int32),
            buf(wide_rows, BF16), buf(wide_rows, BF16), buf(rows, BF16), buf(rows, BF16),
            buf(prompt_rows, BF16), buf(prompt_rows, BF16),
            buf((HEADS, KV, 16, HD), BF16),
            buf((16, KV, 16, HD), BF16),
            buf((NPROMPT, KV, 2, 16, HD), BF16),
            buf((PLANE, KV, 2, 2, 16, HD), BF16),
            buf((PLANE, KV, 2, 2, 16, HD), BF16),
            buf((8, 128), jnp.int32),
            buf((PLANE, 8, 128), jnp.int32),
            pltpu.SMEM((PLANE, 8, 128), jnp.int32),
            buf((KV, HD, heads_wide), BF16),
            buf((KV, HD, heads_wide), BF16),
            buf((KV, ROWS, heads_wide), F32),
            buf((KV, ROWS, heads_wide), F32),
            buf((KV, HD, heads_wide), F32),
            buf((KV, 8, heads_wide), F32),
            buf((KV, PLEN, heads_wide), BF16),
            buf((KV, PLEN, heads_wide), BF16),
            buf((KV, ROWS, heads_wide), BF16),
            buf((KV, ROWS, heads_wide), BF16),
            buf((KV, HD, heads_wide), BF16),
            buf((KV, 2 * HD, PLEN), BF16),
            buf((KV, PLANE, 2, 2, 16, HD), BF16),
            buf((KV, PLANE, 2, 2, 16, HD), BF16),
            buf((16, KV, 16, HD), BF16),
            buf((16, KV, 16, HD), BF16),
            buf(wide_rows, BF16), buf(wide_rows, BF16), buf(rows, BF16), buf(rows, BF16),
            dma((12,)), dma((8,)), dma,
            dma((16,)), dma((16,)), dma((PLANE,)), dma((PLANE,)),
            dma((PLANE,)), dma((PLANE,)), dma((KV, PLANE)), dma((KV, PLANE)),
            dma((16,)), dma((16,)),
        ],
        compiler_params=pltpu.CompilerParams(
            collective_id=0, has_side_effects=True, vmem_limit_bytes=56 * 1024 * 1024
        ),
        name="attend",
    )(prompt_owner, row_comp, query, comp_key, comp_value, prompt_key, prompt_value, out_grad)
    return pl.pallas_call(
        hand_over,
        out_shape=tuple(like(r) for r in results),
        in_specs=[hbm] * 6,
        out_specs=(hbm,) * 6,
        scratch_shapes=[buf(r.shape, BF16) for r in results] + [dma((18,)), dma((18,))],
        compiler_params=pltpu.CompilerParams(vmem_limit_bytes=60 * 1024 * 1024),
        name="hand_over",
    )(*results)


def solution(mesh):
    placed = (
        P("seq", "head"),
        P("seq", "head"),
        P("seq", "head"),
        P(("seq", "head"), None),
        P(("seq", "head"), None),
        P("seq", "head"),
        P("seq"),
        P(),
    )
    return jax.shard_map(
        shards,
        mesh=mesh,
        in_specs=placed,
        out_specs=(
            P("seq", "head"),
            P("seq", "head"),
            P("seq", "head"),
            P("seq", "head"),
            P(("seq", "head"), None),
            P(("seq", "head"), None),
        ),
        check_vma=False,
    )
```

```python
import math

import jax
import jax.numpy as jnp
from jax import lax
from jax.experimental import pallas as pl
from jax.experimental.pallas import tpu as pltpu
from jax.sharding import PartitionSpec as P

QH = 32
KVH = 8
HD = 128
NPROMPT = 8
PLEN = 256
NGEN = 16
ROWS = 512
GROUP = QH // KVH
HEADS = 4
KV = 2
PLANE = 16
DEPTH = 4
CHUNK = 128
WIDE = GROUP * HD
SPAN = GROUP * CHUNK
CHUNKS = ROWS // CHUNK
MESH = pl.DeviceIdType.MESH
INV_SQRT = 1.0 / math.sqrt(HD)
EXP2_SCALE = INV_SQRT * math.log2(math.e)
NEG_FILL = -1e30
F32 = jnp.float32
BF16 = jnp.bfloat16


def place():
    seq = lax.axis_index("seq")
    head = lax.axis_index("head")
    x, y, z = seq // 16, lax.rem(seq // 4, 4), lax.rem(seq, 4)
    return seq, head, x, y, z, 2 * z + head // 2, lax.rem(head, 2), seq // 8


FAR_Z = (2, 1, 3, 0)
FAR_Z8 = (4, 3, 5, 2, 6, 1, 7, 0)
FAR_XY = sorted(
    ((dx, dy) for dx in range(4) for dy in range(4) if (dx, dy) != (0, 0)),
    key=lambda d: -(min(d[0], 4 - d[0]) + min(d[1], 4 - d[1])),
)


def dot(a, b):
    return jnp.dot(a, b, preferred_element_type=F32)


def wait_bytes(ref, sem):
    pltpu.make_async_copy(ref, ref, sem).wait()


def kernel(
    owner_hbm, comp_hbm, q_hbm, k_hbm, v_hbm, pk_hbm, pv_hbm, g_hbm,
    out_v, qg_v, kg_v, vg_v, finals,
    owner_ref, comp_ref, q_in, g_in, k_in, v_in, pk_in, pv_in,
    own_rows, dense, packed, picked, chosen_kv, info, infos, infos_smem,
    q_turn, g_turn, e_local, p_local, o_local, stats, w_prompt, d_prompt, w_local, d_local, o_turn, pair_turn,
    part, parts, pieces,
    in_sem, local_sem, send_a, recv_a, send_i, recv_i, send_b, recv_b, send_c, recv_c, send_d, recv_d,
):
    seq, head, x, y, z, z8, core, slot = place()
    plane = 4 * x + y
    barrier = pltpu.get_barrier_semaphore()

    served = lax.rem(z8 - slot + 8, 8)
    column = 4 * (served // 2) + 2 * lax.rem(served, 2) + lax.rem(y, 2)
    own = column == plane
    self_slot = lax.rem(z8 - slot + 8, 8) == slot

    def spread_target(dz, other_head):
        return column * DEPTH + lax.rem(z + dz, DEPTH), jnp.int32(other_head)

    def holder(off, k):
        other_slot = lax.rem(z8 + off - slot + 8, 8)
        other_z8 = lax.rem(z8 + off, 8)
        other_y = 2 * lax.rem(other_slot, 2) + lax.rem(y, 2)
        other = 16 * (other_slot // 2) + 4 * other_y + other_z8 // 2
        return other_slot, other, 2 * lax.rem(other_z8, 2) + k

    def xy_peer(d):
        return 4 * lax.rem(x + d[0], 4) + lax.rem(y + d[1], 4)

    def signal(other, other_head):
        pl.semaphore_signal(barrier, inc=1, device_id=(other, other_head), device_id_type=MESH)

    def greet_holder(off):
        for k in range(2):
            _, other, other_head = holder(off, k)
            if off:
                signal(other, other_head)
            else:
                @pl.when(jnp.logical_not(jnp.logical_and(self_slot, core == k)))
                def _():
                    signal(other, other_head)

    small = [
        pltpu.make_async_copy(pk_hbm, pk_in, in_sem.at[0]),
        pltpu.make_async_copy(pv_hbm, pv_in, in_sem.at[1]),
        pltpu.make_async_copy(owner_hbm, owner_ref, in_sem.at[10]),
        pltpu.make_async_copy(comp_hbm, comp_ref, in_sem.at[11]),
    ]
    for load in small:
        load.start()
    for off in FAR_Z8:
        greet_holder(off)
    for d in FAR_XY:
        signal(xy_peer(d) * DEPTH + z, head)

    loads = []
    for kv in range(KV):
        wide, narrow = pl.ds(kv * WIDE, WIDE), pl.ds(kv * HD, HD)
        for n, (src, dst, cols) in enumerate(
            ((q_hbm, q_in, wide), (k_hbm, k_in, narrow), (g_hbm, g_in, wide), (v_hbm, v_in, narrow))
        ):
            loads.append(pltpu.make_async_copy(src.at[:, cols], dst.at[kv], in_sem.at[2 + 4 * kv + n]))
    for load in loads:
        load.start()
    for load in small:
        load.wait()

    both = jnp.concatenate([pk_in[...].astype(F32), pv_in[...].astype(F32)], 0).astype(BF16)
    for other_head in range(HEADS):
        for kv in range(KV):
            lo = (KV * other_head + kv) * HD
            own_rows[other_head, kv] = both[:, lo : lo + HD]

    lead_comp = comp_ref[0]
    lead = owner_ref[lead_comp // NGEN]
    tail = owner_ref[comp_ref[ROWS - 1] // NGEN]
    split = jnp.int32(0)
    for step in (256, 128, 64, 32, 16, 8, 4, 2, 1):
        split = jnp.where(comp_ref[split + step - 1] == lead_comp, split + step, split)
    info[...] = jnp.where(lax.broadcasted_iota(jnp.int32, (8, 128), 0) < 4, lead, tail)
    infos[plane] = info[...]

    def loop(lo, hi, body):
        def step(i, carry):
            body(i)
            return carry

        lax.fori_loop(lo, hi, step, 0)

    lane_row = lax.broadcasted_iota(jnp.int32, (1, SPAN), 1) % CHUNK

    def before(kv):
        values_t = v_in[kv].T
        for chunk in range(CHUNKS):
            lo, hi = chunk * CHUNK, (chunk + 1) * CHUNK
            span = slice(chunk * SPAN, (chunk + 1) * SPAN)
            q_t = jnp.concatenate([q_in[kv, lo:hi, j * HD : (j + 1) * HD].T for j in range(GROUP)], 1)
            g_t = jnp.concatenate([g_in[kv, lo:hi, j * HD : (j + 1) * HD].T for j in range(GROUP)], 1)
            q_turn[kv, :, span] = q_t
            g_turn[kv, :, span] = g_t
            key_at = lax.broadcasted_iota(jnp.int32, (hi, CHUNK), 0)
            row_at = lo + lax.broadcasted_iota(jnp.int32, (hi, CHUNK), 1)
            seen = jnp.logical_and(key_at <= row_at, jnp.logical_or(key_at >= split, row_at < split))
            bias = jnp.where(seen, 0.0, NEG_FILL)
            scores = dot(k_in[kv, :hi], q_t) + jnp.concatenate([bias] * GROUP, 1)
            top = jnp.max(scores, axis=0, keepdims=True)
            raw = jnp.exp2((scores - top) * EXP2_SCALE)
            e_local[kv, :hi, span] = raw
            o_local[kv, :, span] = dot(values_t[:, :hi], raw.astype(BF16))
            stats[kv, 0:1, span] = top
            stats[kv, 1:2, span] = jnp.sum(raw, axis=0, keepdims=True)
            p_local[kv, :hi, span] = dot(v_in[kv, :hi], g_t)

    def pair_of(turned, is_lead):
        zero = jnp.zeros_like(turned)
        return jnp.concatenate([jnp.where(is_lead, turned, zero), jnp.where(is_lead, zero, turned)], 0)

    def stacked(ref, kv):
        return jnp.concatenate(
            [
                ref[kv, c * CHUNK : (c + 1) * CHUNK, j * HD : (j + 1) * HD]
                for c in range(CHUNKS)
                for j in range(GROUP)
            ],
            0,
        )

    def stacked_pair(ref, kv):
        rows = stacked(ref, kv)
        at = lax.broadcasted_iota(jnp.int32, (GROUP * ROWS, 1), 0)
        in_lead = (at // SPAN) * CHUNK + at % CHUNK < split
        zero = jnp.zeros_like(rows)
        return jnp.concatenate([jnp.where(in_lead, rows, zero), jnp.where(in_lead, zero, rows)], 1)

    def middle(kv):
        key_pair = jnp.concatenate([chosen_kv[kv, :, t, 0].reshape(PLEN, HD) for t in range(2)], 1)
        value_pair = jnp.concatenate([chosen_kv[kv, :, t, 1].reshape(PLEN, HD) for t in range(2)], 1)
        pair_turn[kv] = key_pair.T
        value_pair_t = value_pair.T
        spans = [slice(c * SPAN, (c + 1) * SPAN) for c in range(CHUNKS)]
        leads = [c * CHUNK + lane_row < split for c in range(CHUNKS)]

        def products(c):
            return (
                dot(key_pair, pair_of(q_turn[kv, :, spans[c]], leads[c])),
                dot(value_pair, pair_of(g_turn[kv, :, spans[c]], leads[c])),
            )

        def weigh(c, s_prompt):
            span = spans[c]
            top_local = stats[kv, 0:1, span]
            top = jnp.maximum(top_local, jnp.max(s_prompt, axis=0, keepdims=True))
            e_prompt = jnp.exp2((s_prompt - top) * EXP2_SCALE)
            rescale = jnp.exp2((top_local - top) * EXP2_SCALE)
            inv = 1.0 / (jnp.sum(e_prompt, axis=0, keepdims=True) + rescale * stats[kv, 1:2, span])
            rescale = rescale * inv
            e_prompt = e_prompt * inv
            wh_prompt = e_prompt.astype(BF16)
            w_prompt[kv, :, span] = wh_prompt
            stats[kv, 2:3, span] = rescale
            o_pair = dot(value_pair_t, wh_prompt)
            return e_prompt, o_pair, rescale

        def finish(c, e_prompt, o_pair, rescale, p_prompt):
            span = spans[c]
            o_t = jnp.where(leads[c], o_pair[:HD], o_pair[HD:]) + o_local[kv, :, span] * rescale
            o_t = o_t.astype(BF16)
            o_turn[kv, :, span] = o_t
            delta = jnp.sum(o_t.astype(F32) * g_turn[kv, :, span].astype(F32), axis=0, keepdims=True)
            stats[kv, 3:4, span] = delta
            d_prompt[kv, :, span] = (e_prompt * (p_prompt - delta)).astype(BF16)

        ahead = products(0)
        held = None
        for c in range(CHUNKS):
            s_prompt, p_prompt = ahead
            if c + 1 < CHUNKS:
                ahead = products(c + 1)
            weighed = weigh(c, s_prompt)
            if held is not None:
                finish(*held)
            held = (c, *weighed, p_prompt)
        finish(*held)
        dk_pair = dot(d_prompt[kv], stacked_pair(q_in, kv)) * INV_SQRT
        dv_pair = dot(w_prompt[kv], stacked_pair(g_in, kv))
        for t in range(2):
            part[kv, :, t, 0] = dk_pair[:, t * HD : (t + 1) * HD].astype(BF16).reshape(PLANE, 16, HD)
            part[kv, :, t, 1] = dv_pair[:, t * HD : (t + 1) * HD].astype(BF16).reshape(PLANE, 16, HD)

    def after(kv):
        keys_t = k_in[kv].T
        for chunk in range(CHUNKS):
            lo, hi = chunk * CHUNK, (chunk + 1) * CHUNK
            span = slice(chunk * SPAN, (chunk + 1) * SPAN)
            is_lead = lo + lane_row < split
            rescale = stats[kv, 2:3, span]
            delta = stats[kv, 3:4, span]
            weights = e_local[kv, :hi, span] * rescale
            w_local[kv, :hi, span] = weights.astype(BF16)
            ds_local = (weights * (p_local[kv, :hi, span] - delta)).astype(BF16)
            d_local[kv, :hi, span] = ds_local
            dq_pair = dot(pair_turn[kv], d_prompt[kv, :, span])
            dq_t = jnp.where(is_lead, dq_pair[:HD], dq_pair[HD:]) + dot(keys_t[:, :hi], ds_local)
            dq_t = (dq_t * INV_SQRT).astype(BF16)
            o_t = o_turn[kv, :, span]
            for j in range(GROUP):
                cols = slice(j * HD, (j + 1) * HD)
                out_v[kv, lo:hi, cols] = o_t[:, j * CHUNK : (j + 1) * CHUNK].T
                qg_v[kv, lo:hi, cols] = dq_t[:, j * CHUNK : (j + 1) * CHUNK].T
        q_all = stacked(q_in, kv)
        g_all = stacked(g_in, kv)
        for chunk in range(CHUNKS):
            lo, hi = chunk * CHUNK, (chunk + 1) * CHUNK
            start = chunk * SPAN
            kg_v[kv, lo:hi] = (dot(d_local[kv, lo:hi, start:], q_all[start:]) * INV_SQRT).astype(BF16)
            vg_v[kv, lo:hi] = dot(w_local[kv, lo:hi, start:], g_all[start:]).astype(BF16)

    def copy_a(dz, other_head):
        at = 2 * slot + core
        return pltpu.make_async_remote_copy(
            src_ref=own_rows.at[other_head], dst_ref=dense.at[at],
            send_sem=send_a.at[4 * dz + other_head], recv_sem=recv_a.at[at],
            device_id=spread_target(dz, other_head), device_id_type=MESH,
        )

    def self_a(other_head):
        return jnp.logical_and(own, head == other_head)

    def start_a(dz, other_head):
        if dz:
            copy_a(dz, other_head).start()
            return
        at = 2 * slot + core

        @pl.when(self_a(other_head))
        def _():
            pltpu.make_async_copy(own_rows.at[other_head], dense.at[at], recv_a.at[at]).start()

        @pl.when(jnp.logical_not(self_a(other_head)))
        def _():
            copy_a(dz, other_head).start()

    def wait_send_a(dz, other_head):
        if dz:
            copy_a(dz, other_head).wait_send()
            return

        @pl.when(jnp.logical_not(self_a(other_head)))
        def _():
            copy_a(dz, other_head).wait_send()

    def copy_info(n):
        return pltpu.make_async_remote_copy(
            src_ref=info, dst_ref=infos.at[plane], send_sem=send_i.at[n], recv_sem=recv_i.at[plane],
            device_id=(xy_peer(FAR_XY[n]) * DEPTH + z, head), device_id_type=MESH,
        )

    def copy_b(kv, n):
        return pltpu.make_async_remote_copy(
            src_ref=picked.at[kv, n], dst_ref=chosen_kv.at[kv, plane],
            send_sem=send_b.at[kv, n], recv_sem=recv_b.at[kv, plane],
            device_id=(xy_peer(FAR_XY[n]) * DEPTH + z, head), device_id_type=MESH,
        )

    def copy_c(kv, n):
        other = xy_peer(FAR_XY[n])
        return pltpu.make_async_remote_copy(
            src_ref=part.at[kv, other], dst_ref=parts.at[kv, plane],
            send_sem=send_c.at[kv, n], recv_sem=recv_c.at[kv, plane],
            device_id=(other * DEPTH + z, head), device_id_type=MESH,
        )

    def copy_d(off, k):
        other_slot, other, other_head = holder(off, k)
        at = DEPTH * head + z
        return other_slot, pltpu.make_async_remote_copy(
            src_ref=pieces.at[2 * other_slot + k], dst_ref=finals.at[at],
            send_sem=send_d.at[2 * off + k], recv_sem=recv_d.at[at],
            device_id=(other, other_head), device_id_type=MESH,
        )

    def self_d(k):
        return jnp.logical_and(self_slot, core == k)

    def start_d(off, k):
        other_slot, copy = copy_d(off, k)
        if off:
            copy.start()
            return
        at = DEPTH * head + z

        @pl.when(self_d(k))
        def _():
            pltpu.make_async_copy(pieces.at[2 * other_slot + k], finals.at[at], recv_d.at[at]).start()

        @pl.when(jnp.logical_not(self_d(k)))
        def _():
            copy.start()

    def wait_send_d(off, k):
        _, copy = copy_d(off, k)
        if off:
            copy.wait_send()
            return

        @pl.when(jnp.logical_not(self_d(k)))
        def _():
            copy.wait_send()

    @pl.when(self_slot)
    def _():
        pl.semaphore_wait(barrier, 15 + 15)

    @pl.when(jnp.logical_not(self_slot))
    def _():
        pl.semaphore_wait(barrier, 15 + 16)

    for dz in FAR_Z:
        for other_head in range(HEADS):
            start_a(dz, other_head)
    for n in range(PLANE - 1):
        copy_info(n).start()
    for load in loads:
        load.wait()
    loop(0, KV, before)
    for d in FAR_XY:
        other = xy_peer(d)
        wait_bytes(infos.at[other], recv_i.at[other])
    to_smem = pltpu.make_async_copy(infos, infos_smem, local_sem)
    to_smem.start()
    loop(0, 16, lambda i: wait_bytes(dense.at[i], recv_a.at[i]))
    to_smem.wait()
    for p in range(NPROMPT):
        for kv in range(KV):
            first = dense[2 * p, kv].astype(F32)
            second = dense[2 * p + 1, kv].astype(F32)
            packed[p, kv, 0] = jnp.concatenate([first[:8], second[:8]], 0).astype(BF16)
            packed[p, kv, 1] = jnp.concatenate([first[8:], second[8:]], 0).astype(BF16)
    for kv in range(KV):
        for n, d in enumerate(FAR_XY):
            other = xy_peer(d)
            picked[kv, n, 0] = packed[infos_smem[other, 0, 0], kv]
            picked[kv, n, 1] = packed[infos_smem[other, 4, 0], kv]
            copy_b(kv, n).start()
        chosen_kv[kv, plane, 0] = packed[lead, kv]
        chosen_kv[kv, plane, 1] = packed[tail, kv]

    def middle_step(kv):
        for d in FAR_XY:
            other = xy_peer(d)
            wait_bytes(chosen_kv.at[kv, other], recv_b.at[kv, other])
        middle(kv)
        for n in range(PLANE - 1):
            copy_c(kv, n).start()
        parts[kv, plane] = part[kv, plane]

    loop(0, KV, middle_step)

    terms = 2 * PLANE * 16
    lane = lax.broadcasted_iota(jnp.int32, (1, terms), 1)
    lane_slot = jnp.zeros((1, terms), jnp.int32)
    for i in range(PLANE):
        lane_slot = jnp.where(lane // 16 == 2 * i, infos_smem[i, 0, 0], lane_slot)
        lane_slot = jnp.where(lane // 16 == 2 * i + 1, infos_smem[i, 4, 0], lane_slot)
    row = lax.broadcasted_iota(jnp.int32, (NPROMPT * 16, terms), 0)
    lanes = lax.broadcasted_iota(jnp.int32, (NPROMPT * 16, terms), 1)
    chosen = jnp.logical_and(row // 16 == lane_slot, lax.rem(row, 16) == lax.rem(lanes, 16))
    chosen = jnp.where(chosen, 1.0, 0.0).astype(BF16)

    def after_step(kv):
        after(kv)

    loop(0, KV, after_step)

    for kv in range(KV):
        for d in FAR_XY:
            other = xy_peer(d)
            wait_bytes(parts.at[kv, other], recv_c.at[kv, other])
        sums = [dot(chosen, parts[kv, :, :, n].reshape(terms, HD)) for n in range(2)]
        for i in range(2 * NPROMPT):
            lo = 8 * i
            pieces[i, kv] = jnp.concatenate([sums[0][lo : lo + 8], sums[1][lo : lo + 8]], 0).astype(BF16)
    for off in FAR_Z8:
        for k in range(2):
            start_d(off, k)

    for n in range(PLANE - 1):
        copy_info(n).wait_send()
        for kv in range(KV):
            copy_b(kv, n).wait_send()
            copy_c(kv, n).wait_send()
    for dz in FAR_Z:
        for other_head in range(HEADS):
            wait_send_a(dz, other_head)
    for off in FAR_Z8:
        for k in range(2):
            wait_send_d(off, k)
    loop(0, 16, lambda i: wait_bytes(finals.at[i], recv_d.at[i]))


def hand_over(out_v, qg_v, kg_v, vg_v, finals, out_hbm, qg_hbm, kg_hbm, vg_hbm, pkg_ref, pvg_ref, sem):
    copies = []
    for src, dst, width in ((out_v, out_hbm, WIDE), (qg_v, qg_hbm, WIDE), (kg_v, kg_hbm, HD), (vg_v, vg_hbm, HD)):
        for kv in range(KV):
            target = dst.at[:, pl.ds(kv * width, width)]
            copies.append(pltpu.make_async_copy(src.at[kv], target, sem.at[len(copies)]))
    for copy in copies:
        copy.start()
    for other_head in range(HEADS):
        for kv in range(KV):
            total = finals[DEPTH * other_head, kv].astype(F32)
            for other_z in range(1, DEPTH):
                total = total + finals[DEPTH * other_head + other_z, kv].astype(F32)
            lo = (KV * other_head + kv) * HD
            pkg_ref[:, lo : lo + HD] = total[:8].astype(BF16)
            pvg_ref[:, lo : lo + HD] = total[8:].astype(BF16)
    for copy in copies:
        copy.wait()


def shards(query, comp_key, comp_value, prompt_key, prompt_value, out_grad, row_comp, prompt_owner):
    vmem = pl.BlockSpec(memory_space=pltpu.VMEM)
    hbm = pl.BlockSpec(memory_space=pl.ANY)
    dma = pltpu.SemaphoreType.DMA
    wide_rows = (KV, ROWS, WIDE)
    rows = (KV, ROWS, HD)
    heads_wide = GROUP * ROWS
    prompt_rows = prompt_key.shape
    like = lambda a: jax.ShapeDtypeStruct(a.shape, BF16)
    buf = pltpu.VMEM
    results = pl.pallas_call(
        kernel,
        out_shape=(
            buf(wide_rows, BF16), buf(wide_rows, BF16), buf(rows, BF16), buf(rows, BF16),
            buf((16, KV, 16, HD), BF16),
        ),
        in_specs=[hbm] * 8,
        out_specs=(vmem,) * 5,
        scratch_shapes=[
            pltpu.SMEM((NPROMPT,), jnp.int32), pltpu.SMEM((ROWS,), jnp.int32),
            buf(wide_rows, BF16), buf(wide_rows, BF16), buf(rows, BF16), buf(rows, BF16),
            buf(prompt_rows, BF16), buf(prompt_rows, BF16),
            buf((HEADS, KV, 16, HD), BF16),
            buf((16, KV, 16, HD), BF16),
            buf((NPROMPT, KV, 2, 16, HD), BF16),
            buf((KV, PLANE, 2, 2, 16, HD), BF16),
            buf((KV, PLANE, 2, 2, 16, HD), BF16),
            buf((8, 128), jnp.int32),
            buf((PLANE, 8, 128), jnp.int32),
            pltpu.SMEM((PLANE, 8, 128), jnp.int32),
            buf((KV, HD, heads_wide), BF16),
            buf((KV, HD, heads_wide), BF16),
            buf((KV, ROWS, heads_wide), F32),
            buf((KV, ROWS, heads_wide), F32),
            buf((KV, HD, heads_wide), F32),
            buf((KV, 8, heads_wide), F32),
            buf((KV, PLEN, heads_wide), BF16),
            buf((KV, PLEN, heads_wide), BF16),
            buf((KV, ROWS, heads_wide), BF16),
            buf((KV, ROWS, heads_wide), BF16),
            buf((KV, HD, heads_wide), BF16),
            buf((KV, 2 * HD, PLEN), BF16),
            buf((KV, PLANE, 2, 2, 16, HD), BF16),
            buf((KV, PLANE, 2, 2, 16, HD), BF16),
            buf((16, KV, 16, HD), BF16),
            dma((12,)), dma,
            dma((16,)), dma((16,)), dma((PLANE,)), dma((PLANE,)),
            dma((KV, PLANE)), dma((KV, PLANE)), dma((KV, PLANE)), dma((KV, PLANE)),
            dma((16,)), dma((16,)),
        ],
        compiler_params=pltpu.CompilerParams(
            collective_id=0, has_side_effects=True, vmem_limit_bytes=56 * 1024 * 1024
        ),
        name="attend",
    )(prompt_owner, row_comp, query, comp_key, comp_value, prompt_key, prompt_value, out_grad)
    return pl.pallas_call(
        hand_over,
        out_shape=(
            like(query), like(query), like(comp_key), like(comp_value), like(prompt_key), like(prompt_value),
        ),
        in_specs=[hbm] * 4 + [vmem],
        out_specs=(hbm,) * 4 + (vmem, vmem),
        scratch_shapes=[dma((8,))],
        name="hand_over",
    )(*(pltpu.with_memory_space_constraint(r, pltpu.VMEM) for r in results))


def solution(mesh):
    placed = (
        P("seq", "head"),
        P("seq", "head"),
        P("seq", "head"),
        P(("seq", "head"), None),
        P(("seq", "head"), None),
        P("seq", "head"),
        P("seq"),
        P(),
    )
    return jax.shard_map(
        shards,
        mesh=mesh,
        in_specs=placed,
        out_specs=(
            P("seq", "head"),
            P("seq", "head"),
            P("seq", "head"),
            P("seq", "head"),
            P(("seq", "head"), None),
            P(("seq", "head"), None),
        ),
        check_vma=False,
    )
```

```python
import math

import jax
import jax.numpy as jnp
from jax import lax
from jax.experimental import pallas as pl
from jax.experimental.pallas import tpu as pltpu
from jax.sharding import PartitionSpec as P

QH = 32
KVH = 8
HD = 128
NPROMPT = 8
PLEN = 256
NGEN = 16
ROWS = 512
GROUP = QH // KVH
HEADS = 4
KV = 2
PLANE = 16
DEPTH = 4
CHUNK = 128
WIDE = GROUP * HD
SPAN = GROUP * CHUNK
CHUNKS = ROWS // CHUNK
MESH = pl.DeviceIdType.MESH
INV_SQRT = 1.0 / math.sqrt(HD)
EXP2_SCALE = INV_SQRT * math.log2(math.e)
NEG_FILL = -1e30
F32 = jnp.float32
BF16 = jnp.bfloat16


def place():
    seq = lax.axis_index("seq")
    head = lax.axis_index("head")
    x, y, z = seq // 16, lax.rem(seq // 4, 4), lax.rem(seq, 4)
    return seq, head, x, y, z, 2 * z + head // 2, lax.rem(head, 2), seq // 8


FAR_Z = (2, 1, 3, 0)
FAR_Z8 = (4, 3, 5, 2, 6, 1, 7, 0)
FAR_XY = sorted(
    ((dx, dy) for dx in range(4) for dy in range(4) if (dx, dy) != (0, 0)),
    key=lambda d: -(min(d[0], 4 - d[0]) + min(d[1], 4 - d[1])),
)


def dot(a, b):
    return jnp.dot(a, b, preferred_element_type=F32)


def wait_bytes(ref, sem):
    pltpu.make_async_copy(ref, ref, sem).wait()


def kernel(
    owner_hbm, comp_hbm, q_hbm, k_hbm, v_hbm, pk_hbm, pv_hbm, g_hbm,
    out_v, qg_v, kg_v, vg_v, finals,
    owner_ref, comp_ref, q_in, g_in, k_in, v_in, pk_in, pv_in,
    own_rows, dense, packed, picked, chosen_kv, info, infos, infos_smem,
    q_pair_turn, g_pair_turn, q_pair, g_pair, e_local, p_local, o_local, stats, w_prompt, d_prompt, w_local, d_local, key_pair_turn, value_pair_turn,
    part, parts, pieces,
    in_sem, local_sem, send_a, recv_a, send_i, recv_i, send_b, recv_b, send_c, recv_c, send_d, recv_d,
):
    seq, head, x, y, z, z8, core, slot = place()
    plane = 4 * x + y
    barrier = pltpu.get_barrier_semaphore()

    served = lax.rem(z8 - slot + 8, 8)
    column = 4 * (served // 2) + 2 * lax.rem(served, 2) + lax.rem(y, 2)
    own = column == plane
    self_slot = lax.rem(z8 - slot + 8, 8) == slot

    def spread_target(dz, other_head):
        return column * DEPTH + lax.rem(z + dz, DEPTH), jnp.int32(other_head)

    def holder(off, k):
        other_slot = lax.rem(z8 + off - slot + 8, 8)
        other_z8 = lax.rem(z8 + off, 8)
        other_y = 2 * lax.rem(other_slot, 2) + lax.rem(y, 2)
        other = 16 * (other_slot // 2) + 4 * other_y + other_z8 // 2
        return other_slot, other, 2 * lax.rem(other_z8, 2) + k

    def xy_peer(d):
        return 4 * lax.rem(x + d[0], 4) + lax.rem(y + d[1], 4)

    def signal(other, other_head):
        pl.semaphore_signal(barrier, inc=1, device_id=(other, other_head), device_id_type=MESH)

    def greet_holder(off):
        for k in range(2):
            _, other, other_head = holder(off, k)
            if off:
                signal(other, other_head)
            else:
                @pl.when(jnp.logical_not(jnp.logical_and(self_slot, core == k)))
                def _():
                    signal(other, other_head)

    small = [
        pltpu.make_async_copy(pk_hbm, pk_in, in_sem.at[0]),
        pltpu.make_async_copy(pv_hbm, pv_in, in_sem.at[1]),
        pltpu.make_async_copy(owner_hbm, owner_ref, in_sem.at[10]),
        pltpu.make_async_copy(comp_hbm, comp_ref, in_sem.at[11]),
    ]
    for load in small:
        load.start()
    for off in FAR_Z8:
        greet_holder(off)
    for d in FAR_XY:
        signal(xy_peer(d) * DEPTH + z, head)

    loads = []
    for kv in range(KV):
        wide, narrow = pl.ds(kv * WIDE, WIDE), pl.ds(kv * HD, HD)
        for n, (src, dst, cols) in enumerate(
            ((q_hbm, q_in, wide), (k_hbm, k_in, narrow), (g_hbm, g_in, wide), (v_hbm, v_in, narrow))
        ):
            loads.append(pltpu.make_async_copy(src.at[:, cols], dst.at[kv], in_sem.at[2 + 4 * kv + n]))
    for load in loads:
        load.start()
    for load in small:
        load.wait()

    both = jnp.concatenate([pk_in[...].astype(F32), pv_in[...].astype(F32)], 0).astype(BF16)
    for other_head in range(HEADS):
        for kv in range(KV):
            lo = (KV * other_head + kv) * HD
            own_rows[other_head, kv] = both[:, lo : lo + HD]

    lead_comp = comp_ref[0]
    lead = owner_ref[lead_comp // NGEN]
    tail = owner_ref[comp_ref[ROWS - 1] // NGEN]
    split = jnp.int32(0)
    for step in (256, 128, 64, 32, 16, 8, 4, 2, 1):
        split = jnp.where(comp_ref[split + step - 1] == lead_comp, split + step, split)
    info[...] = jnp.where(lax.broadcasted_iota(jnp.int32, (8, 128), 0) < 4, lead, tail)
    infos[plane] = info[...]

    def loop(lo, hi, body):
        def step(i, carry):
            body(i)
            return carry

        lax.fori_loop(lo, hi, step, 0)

    lane_row = lax.broadcasted_iota(jnp.int32, (1, SPAN), 1) % CHUNK

    def pair_of(turned, is_lead):
        zero = jnp.zeros_like(turned)
        return jnp.concatenate([jnp.where(is_lead, turned, zero), jnp.where(is_lead, zero, turned)], 0)

    def before(kv):
        values_t = v_in[kv].T
        for chunk in range(CHUNKS):
            lo, hi = chunk * CHUNK, (chunk + 1) * CHUNK
            span = slice(chunk * SPAN, (chunk + 1) * SPAN)
            q_t = jnp.concatenate([q_in[kv, lo:hi, j * HD : (j + 1) * HD].T for j in range(GROUP)], 1)
            g_t = jnp.concatenate([g_in[kv, lo:hi, j * HD : (j + 1) * HD].T for j in range(GROUP)], 1)
            is_lead = lo + lane_row < split
            q_pair_turn[kv, :, span] = pair_of(q_t, is_lead)
            g_pair_turn[kv, :, span] = pair_of(g_t, is_lead)
            lead_rows = lo + lax.broadcasted_iota(jnp.int32, (CHUNK, HD), 0) < split
            lead_rows = jnp.where(lead_rows, 1.0, 0.0).astype(BF16)
            for j in range(GROUP):
                at = slice(chunk * SPAN + j * CHUNK, chunk * SPAN + (j + 1) * CHUNK)
                for src, dst in ((q_in, q_pair), (g_in, g_pair)):
                    block = src[kv, lo:hi, j * HD : (j + 1) * HD]
                    in_lead = block * lead_rows
                    dst[kv, at, :HD] = in_lead
                    dst[kv, at, HD:] = block - in_lead
            key_at = lax.broadcasted_iota(jnp.int32, (hi, CHUNK), 0)
            row_at = lo + lax.broadcasted_iota(jnp.int32, (hi, CHUNK), 1)
            seen = jnp.logical_and(key_at <= row_at, jnp.logical_or(key_at >= split, row_at < split))
            bias = jnp.where(seen, 0.0, NEG_FILL)
            scores = dot(k_in[kv, :hi], q_t) + jnp.concatenate([bias] * GROUP, 1)
            top = jnp.max(scores, axis=0, keepdims=True)
            raw = jnp.exp2((scores - top) * EXP2_SCALE)
            e_local[kv, :hi, span] = raw
            o_local[kv, :, span] = dot(values_t[:, :hi], raw.astype(BF16))
            stats[kv, 0:1, span] = top
            stats[kv, 1:2, span] = jnp.sum(raw, axis=0, keepdims=True)
            grads = dot(v_in[kv, :hi], g_t)
            p_local[kv, :hi, span] = grads
            stats[kv, 4:5, span] = jnp.sum(raw * grads, axis=0, keepdims=True)

    def stacked(ref, kv):
        return jnp.concatenate(
            [
                ref[kv, c * CHUNK : (c + 1) * CHUNK, j * HD : (j + 1) * HD]
                for c in range(CHUNKS)
                for j in range(GROUP)
            ],
            0,
        )

    def middle(kv):
        key_pair = jnp.concatenate([chosen_kv[kv, :, t, 0].reshape(PLEN, HD) for t in range(2)], 1)
        value_pair = jnp.concatenate([chosen_kv[kv, :, t, 1].reshape(PLEN, HD) for t in range(2)], 1)
        key_pair_turn[kv] = key_pair.T
        value_pair_turn[kv] = value_pair.T
        spans = [slice(c * SPAN, (c + 1) * SPAN) for c in range(CHUNKS)]

        def products(c):
            return (
                dot(key_pair, q_pair_turn[kv, :, spans[c]]),
                dot(value_pair, g_pair_turn[kv, :, spans[c]]),
            )

        def weigh(c, s_prompt, p_prompt):
            span = spans[c]
            top_local = stats[kv, 0:1, span]
            top = jnp.maximum(top_local, jnp.max(s_prompt, axis=0, keepdims=True))
            raw = jnp.exp2((s_prompt - top) * EXP2_SCALE)
            rescale = jnp.exp2((top_local - top) * EXP2_SCALE)
            inv = 1.0 / (jnp.sum(raw, axis=0, keepdims=True) + rescale * stats[kv, 1:2, span])
            delta = jnp.sum(raw * p_prompt, axis=0, keepdims=True) + rescale * stats[kv, 4:5, span]
            delta = delta * inv
            weights = raw * inv
            w_prompt[kv, :, span] = weights.astype(BF16)
            d_prompt[kv, :, span] = (weights * (p_prompt - delta)).astype(BF16)
            stats[kv, 2:3, span] = rescale * inv
            stats[kv, 3:4, span] = delta

        half = GROUP * ROWS // 2
        ahead = products(0)
        dk_pair = dv_pair = 0.0
        for c in range(CHUNKS):
            now = ahead
            if c + 1 < CHUNKS:
                ahead = products(c + 1)
            weigh(c, *now)
            if c % 2:
                at = slice((c // 2) * half, (c // 2 + 1) * half)
                dv_pair += dot(w_prompt[kv, :, at], g_pair[kv, at])
                dk_pair += dot(d_prompt[kv, :, at], q_pair[kv, at])
        dk_pair = dk_pair * INV_SQRT
        for t in range(2):
            part[kv, :, t, 0] = dk_pair[:, t * HD : (t + 1) * HD].astype(BF16).reshape(PLANE, 16, HD)
            part[kv, :, t, 1] = dv_pair[:, t * HD : (t + 1) * HD].astype(BF16).reshape(PLANE, 16, HD)

    def after(kv):
        keys_t = k_in[kv].T
        for chunk in range(CHUNKS):
            lo, hi = chunk * CHUNK, (chunk + 1) * CHUNK
            span = slice(chunk * SPAN, (chunk + 1) * SPAN)
            is_lead = lo + lane_row < split
            rescale = stats[kv, 2:3, span]
            delta = stats[kv, 3:4, span]
            weights = e_local[kv, :hi, span] * rescale
            w_local[kv, :hi, span] = weights.astype(BF16)
            ds_local = (weights * (p_local[kv, :hi, span] - delta)).astype(BF16)
            d_local[kv, :hi, span] = ds_local
            dq_pair = dot(key_pair_turn[kv], d_prompt[kv, :, span])
            dq_t = jnp.where(is_lead, dq_pair[:HD], dq_pair[HD:]) + dot(keys_t[:, :hi], ds_local)
            dq_t = (dq_t * INV_SQRT).astype(BF16)
            o_pair = dot(value_pair_turn[kv], w_prompt[kv, :, span])
            o_t = jnp.where(is_lead, o_pair[:HD], o_pair[HD:]) + o_local[kv, :, span] * rescale
            o_t = o_t.astype(BF16)
            for j in range(GROUP):
                cols = slice(j * HD, (j + 1) * HD)
                out_v[kv, lo:hi, cols] = o_t[:, j * CHUNK : (j + 1) * CHUNK].T
                qg_v[kv, lo:hi, cols] = dq_t[:, j * CHUNK : (j + 1) * CHUNK].T
        q_all = stacked(q_in, kv)
        g_all = stacked(g_in, kv)
        for chunk in range(CHUNKS):
            lo, hi = chunk * CHUNK, (chunk + 1) * CHUNK
            start = chunk * SPAN
            kg_v[kv, lo:hi] = (dot(d_local[kv, lo:hi, start:], q_all[start:]) * INV_SQRT).astype(BF16)
            vg_v[kv, lo:hi] = dot(w_local[kv, lo:hi, start:], g_all[start:]).astype(BF16)

    def copy_a(dz, other_head):
        at = 2 * slot + core
        return pltpu.make_async_remote_copy(
            src_ref=own_rows.at[other_head], dst_ref=dense.at[at],
            send_sem=send_a.at[4 * dz + other_head], recv_sem=recv_a.at[at],
            device_id=spread_target(dz, other_head), device_id_type=MESH,
        )

    def self_a(other_head):
        return jnp.logical_and(own, head == other_head)

    def start_a(dz, other_head):
        if dz:
            copy_a(dz, other_head).start()
            return
        at = 2 * slot + core

        @pl.when(self_a(other_head))
        def _():
            pltpu.make_async_copy(own_rows.at[other_head], dense.at[at], recv_a.at[at]).start()

        @pl.when(jnp.logical_not(self_a(other_head)))
        def _():
            copy_a(dz, other_head).start()

    def wait_send_a(dz, other_head):
        if dz:
            copy_a(dz, other_head).wait_send()
            return

        @pl.when(jnp.logical_not(self_a(other_head)))
        def _():
            copy_a(dz, other_head).wait_send()

    def copy_info(n):
        return pltpu.make_async_remote_copy(
            src_ref=info, dst_ref=infos.at[plane], send_sem=send_i.at[n], recv_sem=recv_i.at[plane],
            device_id=(xy_peer(FAR_XY[n]) * DEPTH + z, head), device_id_type=MESH,
        )

    def copy_b(kv, n):
        return pltpu.make_async_remote_copy(
            src_ref=picked.at[kv, n], dst_ref=chosen_kv.at[kv, plane],
            send_sem=send_b.at[kv, n], recv_sem=recv_b.at[kv, plane],
            device_id=(xy_peer(FAR_XY[n]) * DEPTH + z, head), device_id_type=MESH,
        )

    def copy_c(kv, n):
        other = xy_peer(FAR_XY[n])
        return pltpu.make_async_remote_copy(
            src_ref=part.at[kv, other], dst_ref=parts.at[kv, plane],
            send_sem=send_c.at[kv, n], recv_sem=recv_c.at[kv, plane],
            device_id=(other * DEPTH + z, head), device_id_type=MESH,
        )

    def copy_d(off, k):
        other_slot, other, other_head = holder(off, k)
        at = DEPTH * head + z
        return other_slot, pltpu.make_async_remote_copy(
            src_ref=pieces.at[2 * other_slot + k], dst_ref=finals.at[at],
            send_sem=send_d.at[2 * off + k], recv_sem=recv_d.at[at],
            device_id=(other, other_head), device_id_type=MESH,
        )

    def self_d(k):
        return jnp.logical_and(self_slot, core == k)

    def start_d(off, k):
        other_slot, copy = copy_d(off, k)
        if off:
            copy.start()
            return
        at = DEPTH * head + z

        @pl.when(self_d(k))
        def _():
            pltpu.make_async_copy(pieces.at[2 * other_slot + k], finals.at[at], recv_d.at[at]).start()

        @pl.when(jnp.logical_not(self_d(k)))
        def _():
            copy.start()

    def wait_send_d(off, k):
        _, copy = copy_d(off, k)
        if off:
            copy.wait_send()
            return

        @pl.when(jnp.logical_not(self_d(k)))
        def _():
            copy.wait_send()

    @pl.when(self_slot)
    def _():
        pl.semaphore_wait(barrier, 15 + 15)

    @pl.when(jnp.logical_not(self_slot))
    def _():
        pl.semaphore_wait(barrier, 15 + 16)

    for dz in FAR_Z:
        for other_head in range(HEADS):
            start_a(dz, other_head)
    for n in range(PLANE - 1):
        copy_info(n).start()
    for load in loads:
        load.wait()
    loop(0, KV, before)
    for d in FAR_XY:
        other = xy_peer(d)
        wait_bytes(infos.at[other], recv_i.at[other])
    to_smem = pltpu.make_async_copy(infos, infos_smem, local_sem)
    to_smem.start()
    to_smem.wait()

    terms = 2 * PLANE * 16
    lane = lax.broadcasted_iota(jnp.int32, (1, terms), 1)
    lane_slot = jnp.zeros((1, terms), jnp.int32)
    for i in range(PLANE):
        lane_slot = jnp.where(lane // 16 == 2 * i, infos_smem[i, 0, 0], lane_slot)
        lane_slot = jnp.where(lane // 16 == 2 * i + 1, infos_smem[i, 4, 0], lane_slot)
    row = lax.broadcasted_iota(jnp.int32, (NPROMPT * 16, terms), 0)
    lanes = lax.broadcasted_iota(jnp.int32, (NPROMPT * 16, terms), 1)
    chosen = jnp.logical_and(row // 16 == lane_slot, lax.rem(row, 16) == lax.rem(lanes, 16))
    chosen = jnp.where(chosen, 1.0, 0.0).astype(BF16)

    loop(0, 16, lambda i: wait_bytes(dense.at[i], recv_a.at[i]))
    for p in range(NPROMPT):
        for kv in range(KV):
            first = dense[2 * p, kv].astype(F32)
            second = dense[2 * p + 1, kv].astype(F32)
            packed[p, kv, 0] = jnp.concatenate([first[:8], second[:8]], 0).astype(BF16)
            packed[p, kv, 1] = jnp.concatenate([first[8:], second[8:]], 0).astype(BF16)
    for kv in range(KV):
        for n, d in enumerate(FAR_XY):
            other = xy_peer(d)
            picked[kv, n, 0] = packed[infos_smem[other, 0, 0], kv]
            picked[kv, n, 1] = packed[infos_smem[other, 4, 0], kv]
            copy_b(kv, n).start()
        chosen_kv[kv, plane, 0] = packed[lead, kv]
        chosen_kv[kv, plane, 1] = packed[tail, kv]

    def middle_step(kv):
        for d in FAR_XY:
            other = xy_peer(d)
            wait_bytes(chosen_kv.at[kv, other], recv_b.at[kv, other])
        middle(kv)
        for n in range(PLANE - 1):
            copy_c(kv, n).start()
        parts[kv, plane] = part[kv, plane]

    loop(0, KV, middle_step)

    def after_step(kv):
        after(kv)

    loop(0, KV, after_step)

    for kv in range(KV):
        for d in FAR_XY:
            other = xy_peer(d)
            wait_bytes(parts.at[kv, other], recv_c.at[kv, other])
        sums = [dot(chosen, parts[kv, :, :, n].reshape(terms, HD)) for n in range(2)]
        for i in range(2 * NPROMPT):
            lo = 8 * i
            pieces[i, kv] = jnp.concatenate([sums[0][lo : lo + 8], sums[1][lo : lo + 8]], 0).astype(BF16)
    for off in FAR_Z8:
        for k in range(2):
            start_d(off, k)

    for n in range(PLANE - 1):
        copy_info(n).wait_send()
        for kv in range(KV):
            copy_b(kv, n).wait_send()
            copy_c(kv, n).wait_send()
    for dz in FAR_Z:
        for other_head in range(HEADS):
            wait_send_a(dz, other_head)
    for off in FAR_Z8:
        for k in range(2):
            wait_send_d(off, k)
    loop(0, 16, lambda i: wait_bytes(finals.at[i], recv_d.at[i]))


def hand_over(out_v, qg_v, kg_v, vg_v, finals, out_hbm, qg_hbm, kg_hbm, vg_hbm, pkg_hbm, pvg_hbm, pkg_v, pvg_v, sem):
    copies = []
    for src, dst, width in ((out_v, out_hbm, WIDE), (qg_v, qg_hbm, WIDE), (kg_v, kg_hbm, HD), (vg_v, vg_hbm, HD)):
        for kv in range(KV):
            target = dst.at[:, pl.ds(kv * width, width)]
            copies.append(pltpu.make_async_copy(src.at[kv], target, sem.at[len(copies)]))
    for copy in copies:
        copy.start()
    for other_head in range(HEADS):
        for kv in range(KV):
            total = finals[DEPTH * other_head, kv].astype(F32)
            for other_z in range(1, DEPTH):
                total = total + finals[DEPTH * other_head + other_z, kv].astype(F32)
            lo = (KV * other_head + kv) * HD
            pkg_v[:, lo : lo + HD] = total[:8].astype(BF16)
            pvg_v[:, lo : lo + HD] = total[8:].astype(BF16)
    for src, dst in ((pkg_v, pkg_hbm), (pvg_v, pvg_hbm)):
        copies.append(pltpu.make_async_copy(src, dst, sem.at[len(copies)]))
        copies[-1].start()
    for copy in copies:
        copy.wait()


def shards(query, comp_key, comp_value, prompt_key, prompt_value, out_grad, row_comp, prompt_owner):
    vmem = pl.BlockSpec(memory_space=pltpu.VMEM)
    hbm = pl.BlockSpec(memory_space=pl.ANY)
    dma = pltpu.SemaphoreType.DMA
    wide_rows = (KV, ROWS, WIDE)
    rows = (KV, ROWS, HD)
    heads_wide = GROUP * ROWS
    prompt_rows = prompt_key.shape
    like = lambda a: jax.ShapeDtypeStruct(a.shape, BF16)
    buf = pltpu.VMEM
    results = pl.pallas_call(
        kernel,
        out_shape=(
            buf(wide_rows, BF16), buf(wide_rows, BF16), buf(rows, BF16), buf(rows, BF16),
            buf((16, KV, 16, HD), BF16),
        ),
        in_specs=[hbm] * 8,
        out_specs=(vmem,) * 5,
        scratch_shapes=[
            pltpu.SMEM((NPROMPT,), jnp.int32), pltpu.SMEM((ROWS,), jnp.int32),
            buf(wide_rows, BF16), buf(wide_rows, BF16), buf(rows, BF16), buf(rows, BF16),
            buf(prompt_rows, BF16), buf(prompt_rows, BF16),
            buf((HEADS, KV, 16, HD), BF16),
            buf((16, KV, 16, HD), BF16),
            buf((NPROMPT, KV, 2, 16, HD), BF16),
            buf((KV, PLANE, 2, 2, 16, HD), BF16),
            buf((KV, PLANE, 2, 2, 16, HD), BF16),
            buf((8, 128), jnp.int32),
            buf((PLANE, 8, 128), jnp.int32),
            pltpu.SMEM((PLANE, 8, 128), jnp.int32),
            buf((KV, 2 * HD, heads_wide), BF16),
            buf((KV, 2 * HD, heads_wide), BF16),
            buf((KV, heads_wide, 2 * HD), BF16),
            buf((KV, heads_wide, 2 * HD), BF16),
            buf((KV, ROWS, heads_wide), F32),
            buf((KV, ROWS, heads_wide), F32),
            buf((KV, HD, heads_wide), F32),
            buf((KV, 8, heads_wide), F32),
            buf((KV, PLEN, heads_wide), BF16),
            buf((KV, PLEN, heads_wide), BF16),
            buf((KV, ROWS, heads_wide), BF16),
            buf((KV, ROWS, heads_wide), BF16),
            buf((KV, 2 * HD, PLEN), BF16),
            buf((KV, 2 * HD, PLEN), BF16),
            buf((KV, PLANE, 2, 2, 16, HD), BF16),
            buf((KV, PLANE, 2, 2, 16, HD), BF16),
            buf((16, KV, 16, HD), BF16),
            dma((12,)), dma,
            dma((16,)), dma((16,)), dma((PLANE,)), dma((PLANE,)),
            dma((KV, PLANE)), dma((KV, PLANE)), dma((KV, PLANE)), dma((KV, PLANE)),
            dma((16,)), dma((16,)),
        ],
        compiler_params=pltpu.CompilerParams(
            collective_id=0, has_side_effects=True, vmem_limit_bytes=56 * 1024 * 1024
        ),
        name="attend",
    )(prompt_owner, row_comp, query, comp_key, comp_value, prompt_key, prompt_value, out_grad)
    return pl.pallas_call(
        hand_over,
        out_shape=(
            like(query), like(query), like(comp_key), like(comp_value), like(prompt_key), like(prompt_value),
        ),
        in_specs=[hbm] * 4 + [vmem],
        out_specs=(hbm,) * 6,
        scratch_shapes=[buf(prompt_rows, BF16), buf(prompt_rows, BF16), dma((10,))],
        name="hand_over",
    )(*(pltpu.with_memory_space_constraint(r, pltpu.VMEM) for r in results))


def solution(mesh):
    placed = (
        P("seq", "head"),
        P("seq", "head"),
        P("seq", "head"),
        P(("seq", "head"), None),
        P(("seq", "head"), None),
        P("seq", "head"),
        P("seq"),
        P(),
    )
    return jax.shard_map(
        shards,
        mesh=mesh,
        in_specs=placed,
        out_specs=(
            P("seq", "head"),
            P("seq", "head"),
            P("seq", "head"),
            P("seq", "head"),
            P(("seq", "head"), None),
            P(("seq", "head"), None),
        ),
        check_vma=False,
    )
```

```python
import math

import jax
import jax.numpy as jnp
from jax import lax
from jax.experimental import pallas as pl
from jax.experimental.pallas import tpu as pltpu
from jax.sharding import PartitionSpec as P

QH = 32
KVH = 8
HD = 128
NPROMPT = 8
PLEN = 256
NGEN = 16
ROWS = 512
GROUP = QH // KVH
HEADS = 4
KV = 2
PLANE = 16
DEPTH = 4
CHUNK = 128
WIDE = GROUP * HD
SPAN = GROUP * CHUNK
CHUNKS = ROWS // CHUNK
MESH = pl.DeviceIdType.MESH
INV_SQRT = 1.0 / math.sqrt(HD)
EXP2_SCALE = INV_SQRT * math.log2(math.e)
NEG_FILL = -1e30
F32 = jnp.float32
BF16 = jnp.bfloat16


def place():
    seq = lax.axis_index("seq")
    head = lax.axis_index("head")
    x, y, z = seq // 16, lax.rem(seq // 4, 4), lax.rem(seq, 4)
    return seq, head, x, y, z, 2 * z + head // 2, lax.rem(head, 2), seq // 8


FAR_Z = (2, 1, 3, 0)
FAR_Z8 = (4, 3, 5, 2, 6, 1, 7, 0)
FAR_XY = sorted(
    ((dx, dy) for dx in range(4) for dy in range(4) if (dx, dy) != (0, 0)),
    key=lambda d: -(min(d[0], 4 - d[0]) + min(d[1], 4 - d[1])),
)


def dot(a, b):
    return jnp.dot(a, b, preferred_element_type=F32)


def wait_bytes(ref, sem):
    pltpu.make_async_copy(ref, ref, sem).wait()


def kernel(
    owner_hbm, comp_hbm, q_hbm, k_hbm, v_hbm, pk_hbm, pv_hbm, g_hbm,
    out_v, qg_v, kg_v, vg_v, finals,
    owner_ref, comp_ref, q_in, g_in, k_in, v_in, pk_in, pv_in,
    own_rows, dense, packed, picked, chosen_kv, info, infos, infos_smem,
    q_pair_turn, g_pair_turn, q_pair, g_pair, e_local, p_local, o_local, stats, w_prompt, d_prompt, w_local, d_local, key_pair_turn, value_pair_turn,
    part, parts, pieces,
    in_sem, local_sem, send_a, recv_a, send_i, recv_i, send_b, recv_b, send_c, recv_c, send_d, recv_d,
):
    seq, head, x, y, z, z8, core, slot = place()
    plane = 4 * x + y
    barrier = pltpu.get_barrier_semaphore()

    served = lax.rem(z8 - slot + 8, 8)
    column = 4 * (served // 2) + 2 * lax.rem(served, 2) + lax.rem(y, 2)
    own = column == plane
    self_slot = lax.rem(z8 - slot + 8, 8) == slot

    def spread_target(dz, other_head):
        return column * DEPTH + lax.rem(z + dz, DEPTH), jnp.int32(other_head)

    def holder(off, k):
        other_slot = lax.rem(z8 + off - slot + 8, 8)
        other_z8 = lax.rem(z8 + off, 8)
        other_y = 2 * lax.rem(other_slot, 2) + lax.rem(y, 2)
        other = 16 * (other_slot // 2) + 4 * other_y + other_z8 // 2
        return other_slot, other, 2 * lax.rem(other_z8, 2) + k

    def xy_peer(d):
        return 4 * lax.rem(x + d[0], 4) + lax.rem(y + d[1], 4)

    def signal(other, other_head):
        pl.semaphore_signal(barrier, inc=1, device_id=(other, other_head), device_id_type=MESH)

    def greet_holder(off):
        for k in range(2):
            _, other, other_head = holder(off, k)
            if off:
                signal(other, other_head)
            else:
                @pl.when(jnp.logical_not(jnp.logical_and(self_slot, core == k)))
                def _():
                    signal(other, other_head)

    small = [
        pltpu.make_async_copy(pk_hbm, pk_in, in_sem.at[0]),
        pltpu.make_async_copy(pv_hbm, pv_in, in_sem.at[1]),
        pltpu.make_async_copy(owner_hbm, owner_ref, in_sem.at[10]),
        pltpu.make_async_copy(comp_hbm, comp_ref, in_sem.at[11]),
    ]
    for off in FAR_Z8:
        greet_holder(off)
    for load in small:
        load.start()
    for d in FAR_XY:
        signal(xy_peer(d) * DEPTH + z, head)

    loads = []
    for kv in range(KV):
        wide, narrow = pl.ds(kv * WIDE, WIDE), pl.ds(kv * HD, HD)
        for n, (src, dst, cols) in enumerate(
            ((q_hbm, q_in, wide), (k_hbm, k_in, narrow), (g_hbm, g_in, wide), (v_hbm, v_in, narrow))
        ):
            loads.append(pltpu.make_async_copy(src.at[:, cols], dst.at[kv], in_sem.at[2 + 4 * kv + n]))
    for load in loads:
        load.start()
    for load in small:
        load.wait()

    both = jnp.concatenate([pk_in[...].astype(F32), pv_in[...].astype(F32)], 0).astype(BF16)
    for other_head in range(HEADS):
        for kv in range(KV):
            lo = (KV * other_head + kv) * HD
            own_rows[other_head, kv] = both[:, lo : lo + HD]

    lead_comp = comp_ref[0]
    lead = owner_ref[lead_comp // NGEN]
    tail = owner_ref[comp_ref[ROWS - 1] // NGEN]
    split = jnp.int32(0)
    for step in (256, 128, 64, 32, 16, 8, 4, 2, 1):
        split = jnp.where(comp_ref[split + step - 1] == lead_comp, split + step, split)
    info[...] = jnp.where(lax.broadcasted_iota(jnp.int32, (8, 128), 0) < 4, lead, tail)
    infos[plane] = info[...]

    def loop(lo, hi, body):
        def step(i, carry):
            body(i)
            return carry

        lax.fori_loop(lo, hi, step, 0)

    lane_row = lax.broadcasted_iota(jnp.int32, (1, SPAN), 1) % CHUNK

    def pair_of(turned, is_lead):
        zero = jnp.zeros_like(turned)
        return jnp.concatenate([jnp.where(is_lead, turned, zero), jnp.where(is_lead, zero, turned)], 0)

    def before(kv):
        values_t = v_in[kv].T
        for chunk in range(CHUNKS):
            lo, hi = chunk * CHUNK, (chunk + 1) * CHUNK
            span = slice(chunk * SPAN, (chunk + 1) * SPAN)
            q_t = jnp.concatenate([q_in[kv, lo:hi, j * HD : (j + 1) * HD].T for j in range(GROUP)], 1)
            g_t = jnp.concatenate([g_in[kv, lo:hi, j * HD : (j + 1) * HD].T for j in range(GROUP)], 1)
            is_lead = lo + lane_row < split
            q_pair_turn[kv, :, span] = pair_of(q_t, is_lead)
            g_pair_turn[kv, :, span] = pair_of(g_t, is_lead)
            lead_rows = lo + lax.broadcasted_iota(jnp.int32, (CHUNK, HD), 0) < split
            lead_rows = jnp.where(lead_rows, 1.0, 0.0).astype(BF16)
            for j in range(GROUP):
                at = slice(chunk * SPAN + j * CHUNK, chunk * SPAN + (j + 1) * CHUNK)
                for src, dst in ((q_in, q_pair), (g_in, g_pair)):
                    block = src[kv, lo:hi, j * HD : (j + 1) * HD]
                    in_lead = block * lead_rows
                    dst[kv, at, :HD] = in_lead
                    dst[kv, at, HD:] = block - in_lead
            key_at = lax.broadcasted_iota(jnp.int32, (hi, CHUNK), 0)
            row_at = lo + lax.broadcasted_iota(jnp.int32, (hi, CHUNK), 1)
            seen = jnp.logical_and(key_at <= row_at, jnp.logical_or(key_at >= split, row_at < split))
            bias = jnp.where(seen, 0.0, NEG_FILL)
            scores = dot(k_in[kv, :hi], q_t) + jnp.concatenate([bias] * GROUP, 1)
            top = jnp.max(scores, axis=0, keepdims=True)
            raw = jnp.exp2((scores - top) * EXP2_SCALE)
            e_local[kv, :hi, span] = raw
            o_local[kv, :, span] = dot(values_t[:, :hi], raw.astype(BF16))
            stats[kv, 0:1, span] = top
            stats[kv, 1:2, span] = jnp.sum(raw, axis=0, keepdims=True)
            grads = dot(v_in[kv, :hi], g_t)
            p_local[kv, :hi, span] = grads
            stats[kv, 4:5, span] = jnp.sum(raw * grads, axis=0, keepdims=True)

    def stacked(ref, kv):
        return jnp.concatenate(
            [
                ref[kv, c * CHUNK : (c + 1) * CHUNK, j * HD : (j + 1) * HD]
                for c in range(CHUNKS)
                for j in range(GROUP)
            ],
            0,
        )

    def middle(kv):
        key_pair = jnp.concatenate([chosen_kv[kv, :, t, 0].reshape(PLEN, HD) for t in range(2)], 1)
        value_pair = jnp.concatenate([chosen_kv[kv, :, t, 1].reshape(PLEN, HD) for t in range(2)], 1)
        key_pair_turn[kv] = key_pair.T
        value_pair_turn[kv] = value_pair.T
        spans = [slice(c * SPAN, (c + 1) * SPAN) for c in range(CHUNKS)]

        def products(c):
            return (
                dot(key_pair, q_pair_turn[kv, :, spans[c]]),
                dot(value_pair, g_pair_turn[kv, :, spans[c]]),
            )

        def weigh(c, s_prompt, p_prompt):
            span = spans[c]
            top_local = stats[kv, 0:1, span]
            top = jnp.maximum(top_local, jnp.max(s_prompt, axis=0, keepdims=True))
            raw = jnp.exp2((s_prompt - top) * EXP2_SCALE)
            rescale = jnp.exp2((top_local - top) * EXP2_SCALE)
            inv = 1.0 / (jnp.sum(raw, axis=0, keepdims=True) + rescale * stats[kv, 1:2, span])
            delta = jnp.sum(raw * p_prompt, axis=0, keepdims=True) + rescale * stats[kv, 4:5, span]
            delta = delta * inv
            weights = raw * inv
            w_prompt[kv, :, span] = weights.astype(BF16)
            d_prompt[kv, :, span] = (weights * (p_prompt - delta)).astype(BF16)
            stats[kv, 2:3, span] = rescale * inv
            stats[kv, 3:4, span] = delta

        half = GROUP * ROWS // 2
        ahead = products(0)
        dk_pair = dv_pair = 0.0
        for c in range(CHUNKS):
            now = ahead
            if c + 1 < CHUNKS:
                ahead = products(c + 1)
            weigh(c, *now)
            if c % 2:
                at = slice((c // 2) * half, (c // 2 + 1) * half)
                dv_pair += dot(w_prompt[kv, :, at], g_pair[kv, at])
                dk_pair += dot(d_prompt[kv, :, at], q_pair[kv, at])
        dk_pair = dk_pair * INV_SQRT
        for t in range(2):
            part[kv, :, t, 0] = dk_pair[:, t * HD : (t + 1) * HD].astype(BF16).reshape(PLANE, 16, HD)
            part[kv, :, t, 1] = dv_pair[:, t * HD : (t + 1) * HD].astype(BF16).reshape(PLANE, 16, HD)

    def after(kv):
        keys_t = k_in[kv].T
        for chunk in range(CHUNKS):
            lo, hi = chunk * CHUNK, (chunk + 1) * CHUNK
            span = slice(chunk * SPAN, (chunk + 1) * SPAN)
            is_lead = lo + lane_row < split
            rescale = stats[kv, 2:3, span]
            delta = stats[kv, 3:4, span]
            weights = e_local[kv, :hi, span] * rescale
            w_local[kv, :hi, span] = weights.astype(BF16)
            ds_local = (weights * (p_local[kv, :hi, span] - delta)).astype(BF16)
            d_local[kv, :hi, span] = ds_local
            dq_pair = dot(key_pair_turn[kv], d_prompt[kv, :, span])
            dq_t = jnp.where(is_lead, dq_pair[:HD], dq_pair[HD:]) + dot(keys_t[:, :hi], ds_local)
            dq_t = (dq_t * INV_SQRT).astype(BF16)
            o_pair = dot(value_pair_turn[kv], w_prompt[kv, :, span])
            o_t = jnp.where(is_lead, o_pair[:HD], o_pair[HD:]) + o_local[kv, :, span] * rescale
            o_t = o_t.astype(BF16)
            for j in range(GROUP):
                cols = slice(j * HD, (j + 1) * HD)
                out_v[kv, lo:hi, cols] = o_t[:, j * CHUNK : (j + 1) * CHUNK].T
                qg_v[kv, lo:hi, cols] = dq_t[:, j * CHUNK : (j + 1) * CHUNK].T
        q_all = stacked(q_in, kv)
        g_all = stacked(g_in, kv)
        for chunk in range(CHUNKS):
            lo, hi = chunk * CHUNK, (chunk + 1) * CHUNK
            start = chunk * SPAN
            kg_v[kv, lo:hi] = (dot(d_local[kv, lo:hi, start:], q_all[start:]) * INV_SQRT).astype(BF16)
            vg_v[kv, lo:hi] = dot(w_local[kv, lo:hi, start:], g_all[start:]).astype(BF16)

    def copy_a(dz, other_head):
        at = 2 * slot + core
        return pltpu.make_async_remote_copy(
            src_ref=own_rows.at[other_head], dst_ref=dense.at[at],
            send_sem=send_a.at[4 * dz + other_head], recv_sem=recv_a,
            device_id=spread_target(dz, other_head), device_id_type=MESH,
        )

    def self_a(other_head):
        return jnp.logical_and(own, head == other_head)

    def start_a(dz, other_head):
        if dz:
            copy_a(dz, other_head).start()
            return
        at = 2 * slot + core

        @pl.when(self_a(other_head))
        def _():
            pltpu.make_async_copy(own_rows.at[other_head], dense.at[at], recv_a).start()

        @pl.when(jnp.logical_not(self_a(other_head)))
        def _():
            copy_a(dz, other_head).start()

    def wait_send_a(dz, other_head):
        if dz:
            copy_a(dz, other_head).wait_send()
            return

        @pl.when(jnp.logical_not(self_a(other_head)))
        def _():
            copy_a(dz, other_head).wait_send()

    def copy_info(n):
        return pltpu.make_async_remote_copy(
            src_ref=info, dst_ref=infos.at[plane], send_sem=send_i.at[n], recv_sem=recv_i,
            device_id=(xy_peer(FAR_XY[n]) * DEPTH + z, head), device_id_type=MESH,
        )

    def copy_b(kv, n):
        return pltpu.make_async_remote_copy(
            src_ref=picked.at[kv, n], dst_ref=chosen_kv.at[kv, plane],
            send_sem=send_b.at[kv, n], recv_sem=recv_b.at[kv],
            device_id=(xy_peer(FAR_XY[n]) * DEPTH + z, head), device_id_type=MESH,
        )

    def copy_c(kv, n):
        other = xy_peer(FAR_XY[n])
        return pltpu.make_async_remote_copy(
            src_ref=part.at[kv, other], dst_ref=parts.at[kv, plane],
            send_sem=send_c.at[kv, n], recv_sem=recv_c.at[kv],
            device_id=(other * DEPTH + z, head), device_id_type=MESH,
        )

    def copy_d(off, k):
        other_slot, other, other_head = holder(off, k)
        at = DEPTH * head + z
        return other_slot, pltpu.make_async_remote_copy(
            src_ref=pieces.at[2 * other_slot + k], dst_ref=finals.at[at],
            send_sem=send_d.at[2 * off + k], recv_sem=recv_d,
            device_id=(other, other_head), device_id_type=MESH,
        )

    def self_d(k):
        return jnp.logical_and(self_slot, core == k)

    def start_d(off, k):
        other_slot, copy = copy_d(off, k)
        if off:
            copy.start()
            return
        at = DEPTH * head + z

        @pl.when(self_d(k))
        def _():
            pltpu.make_async_copy(pieces.at[2 * other_slot + k], finals.at[at], recv_d).start()

        @pl.when(jnp.logical_not(self_d(k)))
        def _():
            copy.start()

    def wait_send_d(off, k):
        _, copy = copy_d(off, k)
        if off:
            copy.wait_send()
            return

        @pl.when(jnp.logical_not(self_d(k)))
        def _():
            copy.wait_send()

    @pl.when(self_slot)
    def _():
        pl.semaphore_wait(barrier, 15 + 15)

    @pl.when(jnp.logical_not(self_slot))
    def _():
        pl.semaphore_wait(barrier, 15 + 16)

    for dz in FAR_Z:
        for other_head in range(HEADS):
            start_a(dz, other_head)
    for n in range(PLANE - 1):
        copy_info(n).start()
    for load in loads:
        load.wait()
    loop(0, KV, before)
    wait_bytes(infos.at[pl.ds(0, PLANE - 1)], recv_i)
    to_smem = pltpu.make_async_copy(infos, infos_smem, local_sem)
    to_smem.start()
    to_smem.wait()

    terms = 2 * PLANE * 16
    lane = lax.broadcasted_iota(jnp.int32, (1, terms), 1)
    lane_slot = jnp.zeros((1, terms), jnp.int32)
    for i in range(PLANE):
        lane_slot = jnp.where(lane // 16 == 2 * i, infos_smem[i, 0, 0], lane_slot)
        lane_slot = jnp.where(lane // 16 == 2 * i + 1, infos_smem[i, 4, 0], lane_slot)
    row = lax.broadcasted_iota(jnp.int32, (NPROMPT * 16, terms), 0)
    lanes = lax.broadcasted_iota(jnp.int32, (NPROMPT * 16, terms), 1)
    chosen = jnp.logical_and(row // 16 == lane_slot, lax.rem(row, 16) == lax.rem(lanes, 16))
    chosen = jnp.where(chosen, 1.0, 0.0).astype(BF16)

    wait_bytes(dense, recv_a)
    for p in range(NPROMPT):
        for kv in range(KV):
            first = dense[2 * p, kv].astype(F32)
            second = dense[2 * p + 1, kv].astype(F32)
            packed[p, kv, 0] = jnp.concatenate([first[:8], second[:8]], 0).astype(BF16)
            packed[p, kv, 1] = jnp.concatenate([first[8:], second[8:]], 0).astype(BF16)
    for kv in range(KV):
        for n, d in enumerate(FAR_XY):
            other = xy_peer(d)
            picked[kv, n, 0] = packed[infos_smem[other, 0, 0], kv]
            picked[kv, n, 1] = packed[infos_smem[other, 4, 0], kv]
            copy_b(kv, n).start()
        chosen_kv[kv, plane, 0] = packed[lead, kv]
        chosen_kv[kv, plane, 1] = packed[tail, kv]

    def middle_step(kv):
        wait_bytes(chosen_kv.at[kv, pl.ds(0, PLANE - 1)], recv_b.at[kv])
        middle(kv)
        for n in range(PLANE - 1):
            copy_c(kv, n).start()
        parts[kv, plane] = part[kv, plane]

    loop(0, KV, middle_step)

    def after_step(kv):
        after(kv)

    loop(0, KV, after_step)

    for kv in range(KV):
        wait_bytes(parts.at[kv, pl.ds(0, PLANE - 1)], recv_c.at[kv])
        sums = [dot(chosen, parts[kv, :, :, n].reshape(terms, HD)) for n in range(2)]
        for i in range(2 * NPROMPT):
            lo = 8 * i
            pieces[i, kv] = jnp.concatenate([sums[0][lo : lo + 8], sums[1][lo : lo + 8]], 0).astype(BF16)
    for off in FAR_Z8:
        for k in range(2):
            start_d(off, k)

    for n in range(PLANE - 1):
        copy_info(n).wait_send()
        for kv in range(KV):
            copy_b(kv, n).wait_send()
            copy_c(kv, n).wait_send()
    for dz in FAR_Z:
        for other_head in range(HEADS):
            wait_send_a(dz, other_head)
    for off in FAR_Z8:
        for k in range(2):
            wait_send_d(off, k)
    wait_bytes(finals, recv_d)


def hand_over(out_v, qg_v, kg_v, vg_v, finals, out_hbm, qg_hbm, kg_hbm, vg_hbm, pkg_hbm, pvg_hbm, pkg_v, pvg_v, sem):
    copies = []
    for src, dst, width in ((out_v, out_hbm, WIDE), (qg_v, qg_hbm, WIDE), (kg_v, kg_hbm, HD), (vg_v, vg_hbm, HD)):
        for kv in range(KV):
            target = dst.at[:, pl.ds(kv * width, width)]
            copies.append(pltpu.make_async_copy(src.at[kv], target, sem.at[len(copies)]))
    for copy in copies:
        copy.start()
    for other_head in range(HEADS):
        for kv in range(KV):
            total = finals[DEPTH * other_head, kv].astype(F32)
            for other_z in range(1, DEPTH):
                total = total + finals[DEPTH * other_head + other_z, kv].astype(F32)
            lo = (KV * other_head + kv) * HD
            pkg_v[:, lo : lo + HD] = total[:8].astype(BF16)
            pvg_v[:, lo : lo + HD] = total[8:].astype(BF16)
    for src, dst in ((pkg_v, pkg_hbm), (pvg_v, pvg_hbm)):
        copies.append(pltpu.make_async_copy(src, dst, sem.at[len(copies)]))
        copies[-1].start()
    for copy in copies:
        copy.wait()


def shards(query, comp_key, comp_value, prompt_key, prompt_value, out_grad, row_comp, prompt_owner):
    vmem = pl.BlockSpec(memory_space=pltpu.VMEM)
    hbm = pl.BlockSpec(memory_space=pl.ANY)
    dma = pltpu.SemaphoreType.DMA
    wide_rows = (KV, ROWS, WIDE)
    rows = (KV, ROWS, HD)
    heads_wide = GROUP * ROWS
    prompt_rows = prompt_key.shape
    like = lambda a: jax.ShapeDtypeStruct(a.shape, BF16)
    buf = pltpu.VMEM
    results = pl.pallas_call(
        kernel,
        out_shape=(
            buf(wide_rows, BF16), buf(wide_rows, BF16), buf(rows, BF16), buf(rows, BF16),
            buf((16, KV, 16, HD), BF16),
        ),
        in_specs=[hbm] * 8,
        out_specs=(vmem,) * 5,
        scratch_shapes=[
            pltpu.SMEM((NPROMPT,), jnp.int32), pltpu.SMEM((ROWS,), jnp.int32),
            buf(wide_rows, BF16), buf(wide_rows, BF16), buf(rows, BF16), buf(rows, BF16),
            buf(prompt_rows, BF16), buf(prompt_rows, BF16),
            buf((HEADS, KV, 16, HD), BF16),
            buf((16, KV, 16, HD), BF16),
            buf((NPROMPT, KV, 2, 16, HD), BF16),
            buf((KV, PLANE, 2, 2, 16, HD), BF16),
            buf((KV, PLANE, 2, 2, 16, HD), BF16),
            buf((8, 128), jnp.int32),
            buf((PLANE, 8, 128), jnp.int32),
            pltpu.SMEM((PLANE, 8, 128), jnp.int32),
            buf((KV, 2 * HD, heads_wide), BF16),
            buf((KV, 2 * HD, heads_wide), BF16),
            buf((KV, heads_wide, 2 * HD), BF16),
            buf((KV, heads_wide, 2 * HD), BF16),
            buf((KV, ROWS, heads_wide), F32),
            buf((KV, ROWS, heads_wide), F32),
            buf((KV, HD, heads_wide), F32),
            buf((KV, 8, heads_wide), F32),
            buf((KV, PLEN, heads_wide), BF16),
            buf((KV, PLEN, heads_wide), BF16),
            buf((KV, ROWS, heads_wide), BF16),
            buf((KV, ROWS, heads_wide), BF16),
            buf((KV, 2 * HD, PLEN), BF16),
            buf((KV, 2 * HD, PLEN), BF16),
            buf((KV, PLANE, 2, 2, 16, HD), BF16),
            buf((KV, PLANE, 2, 2, 16, HD), BF16),
            buf((16, KV, 16, HD), BF16),
            dma((12,)), dma,
            dma((16,)), dma, dma((PLANE,)), dma,
            dma((KV, PLANE)), dma((KV,)), dma((KV, PLANE)), dma((KV,)),
            dma((16,)), dma,
        ],
        compiler_params=pltpu.CompilerParams(
            collective_id=0, has_side_effects=True, vmem_limit_bytes=56 * 1024 * 1024
        ),
        name="attend",
    )(prompt_owner, row_comp, query, comp_key, comp_value, prompt_key, prompt_value, out_grad)
    return pl.pallas_call(
        hand_over,
        out_shape=(
            like(query), like(query), like(comp_key), like(comp_value), like(prompt_key), like(prompt_value),
        ),
        in_specs=[hbm] * 4 + [vmem],
        out_specs=(hbm,) * 6,
        scratch_shapes=[buf(prompt_rows, BF16), buf(prompt_rows, BF16), dma((10,))],
        name="hand_over",
    )(*(pltpu.with_memory_space_constraint(r, pltpu.VMEM) for r in results))


def solution(mesh):
    placed = (
        P("seq", "head"),
        P("seq", "head"),
        P("seq", "head"),
        P(("seq", "head"), None),
        P(("seq", "head"), None),
        P("seq", "head"),
        P("seq"),
        P(),
    )
    return jax.shard_map(
        shards,
        mesh=mesh,
        in_specs=placed,
        out_specs=(
            P("seq", "head"),
            P("seq", "head"),
            P("seq", "head"),
            P("seq", "head"),
            P(("seq", "head"), None),
            P(("seq", "head"), None),
        ),
        check_vma=False,
    )
```
